256 devices in a mesh: epoch: 8 (over x, y_lo), sky: 32 (over z, y_hi, core).
Axes of the slice: x: 4, y: 4 (y_hi: 2, y_lo: 2; y = y_hi * 2 + y_lo), z: 8, core: 2. Of those that a mesh axis runs over, the one named last changes fastest.
Arguments:
- image: bfloat16 [16, 1536, 2048], P('epoch', 'sky'), may hold values from -400 to 400
- inv_variance: bfloat16 [16, 1536, 2048], P('epoch', 'sky'), may hold values from 0.25 to 4
- psf_rows: float32 [9], replicated, may hold values from 0.05 to 1
- psf_cols: float32 [9], replicated, may hold values from 0.05 to 1
- shift_num: int32 [4, 16], replicated, may hold values from -64 to 64, as said below
Outputs:
- search_map: float32 [1536, 2048], P('sky', 'epoch')
The draws below stay inside these ranges and needn't reach their ends.
Inputs may be any that keep to these rules, and one draw needn't show every extreme that they name: `shift_num`: at level l every entry has magnitude at most 4 * 2 * 2^l, and at each level some entry equals plus and some other entry minus that bound.
All inputs are finite; a program needn't handle non-finite values.
Results may differ from the reference program's by a relative error of at most 0.0024.
Values may be sent and summed in bfloat16 or wider, within the bound.
No kernel may reach another device: no remote copies, remote signals or barrier semaphores. Data moves between devices by JAX's collectives and lax.ppermute only.
A program may use at most 64 MiB of HBM per device.

```python
import math
import jax
import jax.numpy as jnp
from jax import lax

EPOCHS = 16
LEVELS = 4
COLS = 2048
PSF_HALF = 4
DEN = 4
VMAX = 2
ROWS = 1536


def draw_image(key, part):
    key_base = jax.random.fold_in(jax.random.fold_in(key, 11), 0)
    base_values = jax.random.normal(key_base, (EPOCHS, ROWS, COLS), jnp.float32)
    return jnp.clip(base_values, -6.0, 6.0).astype(jnp.bfloat16)


def draw_shift_num(key, part):
    key_raw, key_top, key_low = jax.random.split(jax.random.fold_in(key, 23), 3)
    limits = DEN * VMAX * (2 ** jnp.arange(LEVELS, dtype=jnp.int32))[:, None]
    raw_values = jax.random.randint(key_raw, (LEVELS, EPOCHS), 0, 1 << 20, dtype=jnp.int32)
    values = raw_values % (2 * limits + 1) - limits
    column = jnp.arange(EPOCHS, dtype=jnp.int32)[None, :]
    top_pos = jax.random.randint(key_top, (LEVELS, 1), 0, EPOCHS, dtype=jnp.int32)
    low_pos = (top_pos + 1 + jax.random.randint(key_low, (LEVELS, 1), 0, EPOCHS - 1, dtype=jnp.int32)) % EPOCHS
    values = jnp.where(column == top_pos, limits, jnp.where(column == low_pos, -limits, values))
    return values.astype(jnp.int32)


def levels(stream_key, extent, cuts, least, top_value):
    def one(dim, blocks):
        steps = jax.random.uniform(jax.random.fold_in(jax.random.fold_in(stream_key, 6), dim), (blocks,), jnp.float32, least / len(cuts), top_value / len(cuts))
        return jnp.repeat(jnp.exp(steps), extent[dim] // blocks).reshape((-1,) + (1,) * (len(extent) - dim - 1))

    level = one(*cuts[0])
    for cut in cuts[1:]:
        level = level * one(*cut)
    return level


def setup_inputs(seed: int = 0) -> dict:
    arg_keys = jax.random.split(jax.random.key(seed), 6)
    return {
        "image": draw_image(jax.random.fold_in(arg_keys[5], 71), 0),
        "inv_variance": jnp.clip(jnp.exp(math.log(4.0) - 2.7725887 * jax.random.uniform(arg_keys[1], (EPOCHS, ROWS, COLS), jnp.float32) ** levels(arg_keys[1], (EPOCHS, ROWS, COLS), ((0, 8), (1, 32)), -0.2, 0.2)), 0.25, 4.0).astype(jnp.bfloat16),
        "psf_rows": jnp.clip(jnp.exp(jax.random.uniform(arg_keys[2], (2 * PSF_HALF + 1,), jnp.float32, math.log(0.05), math.log(1.0))), 0.05, 1.0),
        "psf_cols": jnp.clip(jnp.exp(jax.random.uniform(arg_keys[3], (2 * PSF_HALF + 1,), jnp.float32, math.log(0.05), math.log(1.0))), 0.05, 1.0),
        "shift_num": draw_shift_num(jax.random.fold_in(arg_keys[5], 71), 0),
    }


def filter_epoch(pixels, weights_in, psf_rows, psf_cols):
    reach = PSF_HALF
    weighted = pixels * weights_in
    weighted_pad = jnp.pad(weighted, ((reach, reach), (reach, reach)))
    variance_pad = jnp.pad(weights_in, ((reach, reach), (reach, reach)))
    row_count = pixels.shape[0]
    col_count = pixels.shape[1]
    rows_psi = jnp.zeros((row_count, col_count + 2 * reach), jnp.float32)
    rows_phi = jnp.zeros((row_count, col_count + 2 * reach), jnp.float32)
    for offset in range(2 * reach + 1):
        rows_psi = rows_psi + psf_rows[offset] * weighted_pad[offset:offset + row_count, :]
        rows_phi = rows_phi + psf_rows[offset] * psf_rows[offset] * variance_pad[offset:offset + row_count, :]
    psi_map = jnp.zeros((row_count, col_count), jnp.float32)
    phi_map = jnp.zeros((row_count, col_count), jnp.float32)
    for offset in range(2 * reach + 1):
        psi_map = psi_map + psf_cols[offset] * rows_psi[:, offset:offset + col_count]
        phi_map = phi_map + psf_cols[offset] * psf_cols[offset] * rows_phi[:, offset:offset + col_count]
    return jnp.stack([psi_map, phi_map])

def shift_rows(padded, numerators, rim_width):
    row_count = padded.shape[2] - 2 * rim_width
    whole_rows = jnp.floor_divide(numerators, DEN)
    fraction = (numerators - whole_rows * DEN).astype(jnp.float32) / DEN
    start_rows = (rim_width - whole_rows - 1).astype(jnp.int32)

    def take_rows(one_block, start):
        return lax.dynamic_slice_in_dim(one_block, start, row_count + 1, axis=1)
    taken_rows = jax.vmap(take_rows)(padded, start_rows)
    fraction = fraction[:, None, None, None]
    return (1.0 - fraction) * taken_rows[:, :, 1:] + fraction * taken_rows[:, :, :-1]

def reference(image, inv_variance, psf_rows, psf_cols, shift_num):

    def one_epoch(pair):
        return filter_epoch(pair[0].astype(jnp.float32), pair[1].astype(jnp.float32), psf_rows, psf_cols)
    stacks = lax.map(one_epoch, jnp.stack([image, inv_variance], axis=1))
    row_count = stacks.shape[2]
    col_count = stacks.shape[3]
    for level_index in range(LEVELS):
        half_span = 2 ** level_index
        groups = EPOCHS // (2 * half_span)
        rim_width = VMAX * half_span + 1
        paired = stacks.reshape(groups, 2, half_span, 2, row_count, col_count)
        lower_half = paired[:, 0].reshape(groups * half_span, 2, row_count, col_count)
        upper_half = paired[:, 1].reshape(groups * half_span, 2, row_count, col_count)
        numerators = shift_num[level_index].reshape(groups, 2, half_span)
        padded = jnp.pad(upper_half, ((0, 0), (0, 0), (rim_width, rim_width), (0, 0)))
        new_lower = lower_half + shift_rows(padded, numerators[:, 0].reshape(-1), rim_width)
        new_upper = lower_half + shift_rows(padded, numerators[:, 1].reshape(-1), rim_width)
        stacks = jnp.stack([new_lower.reshape(groups, half_span, 2, row_count, col_count), new_upper.reshape(groups, half_span, 2, row_count, col_count)], axis=1)
        stacks = stacks.reshape(EPOCHS, 2, row_count, col_count)
    likelihood = stacks[:, 0] / jnp.sqrt(stacks[:, 1])
    peak_value = lax.optimization_barrier(jnp.max(likelihood, axis=0))
    return peak_value + jnp.log(lax.optimization_barrier(jnp.sum(jnp.exp(likelihood - peak_value[None]), axis=0)))
```

```python
import jax
import jax.numpy as jnp
from jax import lax
from jax.experimental import pallas as pl
from jax.experimental.pallas import tpu as pltpu
from jax.sharding import PartitionSpec as P

EPOCHS = 16
LEVELS = 4
PSF = 9
REACH = 4
PEERS = 8
ROWS = 48
LANES = 128
COLS = 256
EDGE_ROW = 8 * ROWS
SEND_ROWS = 9 * ROWS
HALO = [2 * j + REACH for j in range(EPOCHS)]
HALO_AT = [sum(HALO[:j]) for j in range(EPOCHS)]
HALO_ROWS = sum(HALO)
EDGE_LO = HALO[7]
EDGE_HI = HALO[15]
EDGE_LO_AT = 4 * HALO_ROWS
EDGE_HI_AT = EDGE_LO_AT + EDGE_LO
HALO_SEND = 1280
BASE = 40
SPAN = 128
F32 = jnp.float32
BF16 = jnp.bfloat16


def edge_lane(array, j):
    return 32 * ((j // 2) % 4) + (2 * array + j % 2) * 8


def pack_kernel(where_ref, image_ref, variance_ref, out_ref):
    turn = 32 * (where_ref[0] % 4)
    lane = lax.broadcasted_iota(jnp.int32, (ROWS, LANES), 1)
    for c in range(PEERS):
        edges = jnp.zeros((ROWS, LANES), F32)
        for a, ref in enumerate((image_ref, variance_ref)):
            for i in range(2):
                for t in range(2):
                    row = ((a * 2 + i) * 2 + t) * ROWS
                    out_ref[c, row : row + ROWS, :] = ref[i, :, (2 * c + t) * LANES : (2 * c + t + 1) * LANES]
                picked = jnp.zeros((ROWS, LANES), F32)
                if c > 0:
                    left = ref[i, :, (2 * c - 1) * LANES : 2 * c * LANES].astype(F32)
                    picked = jnp.where(lane >= LANES - REACH, left, picked)
                if c < PEERS - 1:
                    right = ref[i, :, (2 * c + 2) * LANES : (2 * c + 3) * LANES].astype(F32)
                    picked = jnp.where(lane < REACH, right, picked)
                edges = edges + pltpu.roll(picked, (2 * a + i) * 8 + REACH, 1)
        edges = pltpu.roll(edges, turn, 1)
        out_ref[c, EDGE_ROW:SEND_ROWS, :] = edges.astype(BF16)


def halo_kernel(where_ref, got_ref, near_ref, far_ref, wide, near, far):
    core = where_ref[1] % 2

    def take(index, source_row, target_row, height):
        low = wide[index, pl.ds(source_row + core * (ROWS - height), height), :]
        high = wide[index, pl.ds(source_row + (1 - core) * (ROWS - height), height), :]
        far[target_row : target_row + height, :] = low
        near[target_row : target_row + height, :] = high

    for k in range(PEERS):
        wide[k] = got_ref[k, :EDGE_ROW, :].astype(F32)
    for half in range(2):
        total = got_ref[4 * half, EDGE_ROW:SEND_ROWS, :].astype(F32)
        for k in range(4 * half + 1, 4 * half + 4):
            total = total + got_ref[k, EDGE_ROW:SEND_ROWS, :].astype(F32)
        wide[PEERS, half * ROWS : (half + 1) * ROWS, :] = total
    for j in range(EPOCHS):
        for a in range(2):
            for t in range(2):
                row = ((a * 2 + j % 2) * 2 + t) * ROWS
                take(j // 2, row, (a * 2 + t) * HALO_ROWS + HALO_AT[j], HALO[j])
    take(PEERS, 0, EDGE_LO_AT, EDGE_LO)
    take(PEERS, ROWS, EDGE_HI_AT, EDGE_HI)
    rest = EDGE_HI_AT + EDGE_HI
    near[rest:HALO_SEND, :] = jnp.zeros((HALO_SEND - rest, LANES), F32)
    far[rest:HALO_SEND, :] = jnp.zeros((HALO_SEND - rest, LANES), F32)
    near_ref[...] = near[...].astype(BF16)
    far_ref[...] = far[...].astype(BF16)


def split(values):
    high = values.astype(BF16)
    return high, (values - high.astype(F32)).astype(BF16)


def column_filter(image, variance, taps, count):
    high, low = split(image * variance)
    variance = variance.astype(BF16)

    def dot(left, right):
        return jnp.dot(left, right, preferred_element_type=F32)

    psi = dot(high, taps[0]) + (dot(low, taps[0]) + dot(high, taps[1]))
    phi = dot(variance, taps[2]) + dot(variance, taps[3])
    return psi, phi


def own_kernel(cols_ref, got_ref, out_ref, taps_ref, image, variance):
    shape = (COLS + LANES, COLS)
    place = lax.broadcasted_iota(jnp.int32, shape, 0)
    place = jnp.where(place < COLS + LANES // 2, place, place - (COLS + LANES))
    step = place - lax.broadcasted_iota(jnp.int32, shape, 1) + REACH
    psi_taps = jnp.zeros(shape, F32)
    phi_taps = jnp.zeros(shape, F32)
    for b in range(PSF):
        hit = step == b
        psi_taps = jnp.where(hit, cols_ref[b], psi_taps)
        phi_taps = jnp.where(hit, cols_ref[b] * cols_ref[b], phi_taps)
    taps_ref[0], taps_ref[1] = split(psi_taps)
    taps_ref[2], taps_ref[3] = split(phi_taps)
    edges = []
    for half in range(2):
        total = got_ref[4 * half, EDGE_ROW:SEND_ROWS, :].astype(F32)
        for k in range(4 * half + 1, 4 * half + 4):
            total = total + got_ref[k, EDGE_ROW:SEND_ROWS, :].astype(F32)
        edges.append(total)
    for j in range(EPOCHS):
        for a, ref in enumerate((image, variance)):
            for t in range(2):
                row = ((a * 2 + j % 2) * 2 + t) * ROWS
                ref[j * ROWS : (j + 1) * ROWS, t * LANES : (t + 1) * LANES] = got_ref[
                    j // 2, row : row + ROWS, :
                ].astype(F32)
            turn = (LANES - REACH - edge_lane(a, j)) % LANES
            ref[j * ROWS : (j + 1) * ROWS, COLS:] = pltpu.roll(edges[j // 8], turn, 1)
    psi, phi = column_filter(image[...], variance[...], taps_ref, EPOCHS)
    for j in range(EPOCHS):
        rows = slice(j * ROWS, (j + 1) * ROWS)
        for t in range(2):
            lanes = slice(t * LANES, (t + 1) * LANES)
            out_ref[j, t] = psi[rows, lanes]
            out_ref[j, 2 + t] = phi[rows, lanes]


def stack_kernel(
    where_ref,
    rows_ref,
    shift_ref,
    own_ref,
    taps_ref,
    near_ref,
    far_ref,
    out_ref,
    wide,
    image,
    variance,
    filtered,
    maps,
    first,
    second,
):
    sky = where_ref[1]
    core = sky % 2
    wide[core] = near_ref[...].astype(F32)
    wide[1 - core] = far_ref[...].astype(F32)
    for side in range(2):
        source = 1 - side
        for a, ref in enumerate((image, variance)):
            for t in range(2):
                start = (a * 2 + t) * HALO_ROWS
                ref[side * HALO_ROWS : (side + 1) * HALO_ROWS, t * LANES : (t + 1) * LANES] = wide[
                    source, start : start + HALO_ROWS, :
                ]
            for j in range(EPOCHS):
                start, height = (EDGE_LO_AT, EDGE_LO) if j < 8 else (EDGE_HI_AT, EDGE_HI)
                if side == 0:
                    start = start + height - HALO[j]
                turn = (LANES - REACH - edge_lane(a, j)) % LANES
                row = side * HALO_ROWS + HALO_AT[j]
                ref[row : row + HALO[j], COLS:] = pltpu.roll(wide[source, start : start + HALO[j], :], turn, 1)
    psi, phi = column_filter(image[...], variance[...], taps_ref, EPOCHS)
    for t in range(2):
        lanes = slice(t * LANES, (t + 1) * LANES)
        filtered[t] = psi[:, lanes]
        filtered[2 + t] = phi[:, lanes]
    for j in range(EPOCHS):
        for p in range(4):
            above = HALO_AT[j]
            below = HALO_ROWS + HALO_AT[j]
            maps[j, p, BASE - HALO[j] : BASE, :] = filtered[p, above : above + HALO[j], :]
            maps[j, p, BASE : BASE + ROWS, :] = own_ref[j, p]
            maps[j, p, BASE + ROWS : BASE + ROWS + HALO[j], :] = filtered[p, below : below + HALO[j], :]

    def chunks(reach):
        return range((BASE - reach) // 8 * 8, BASE + ROWS + reach, 8)

    row_taps = [[rows_ref[a] for a in range(PSF)], [rows_ref[a] * rows_ref[a] for a in range(PSF)]]

    for j in range(EPOCHS):
        for m in range(2):

            def filter_rows(t, carry, j=j, m=m):
                p = 2 * m + t
                for r in chunks(2 * j):
                    total = row_taps[m][0] * maps[j, p, r - REACH : r - REACH + 8, :]
                    for a in range(1, PSF):
                        total = total + row_taps[m][a] * maps[j, p, r - REACH + a : r - REACH + a + 8, :]
                    first[j, p, r : r + 8, :] = total
                return carry

            lax.fori_loop(0, 2, filter_rows, 0)

    def clear(ref):
        @pl.when(sky == 0)
        def _():
            ref[:, :, :BASE, :] = jnp.zeros((EPOCHS, 4, BASE, LANES), F32)

        @pl.when(sky == sky_last)
        def _():
            ref[:, :, BASE + ROWS :, :] = jnp.zeros((EPOCHS, 4, SPAN - BASE - ROWS, LANES), F32)

    sky_last = where_ref[2] - 1
    clear(first)

    def moves(level, j):
        number = shift_ref[level, j]
        whole = lax.shift_right_arithmetic(number, 2)
        part = number - whole * 4
        fraction = part.astype(F32) * 0.25
        behind = jnp.where(part > 0, whole + 1, whole)
        return whole, behind, 1.0 - fraction, fraction

    def shifted(ref, k, p, r, move):
        whole, behind, keep, fraction = move
        return keep * ref[k, p, pl.ds(r - whole, 8), :] + fraction * ref[k, p, pl.ds(r - behind, 8), :]

    source, target = first, second
    for level in range(LEVELS - 1):
        span = 1 << level
        for low in range(EPOCHS):
            if low & span:
                continue
            high = low + span
            reach = 2 * (low >> (level + 1) << (level + 1))
            to_low, to_high = moves(level, low), moves(level, high)

            def step(p, carry, low=low, high=high, reach=reach, to_low=to_low, to_high=to_high, source=source, target=target):
                for r in chunks(reach):
                    base = source[low, p, r : r + 8, :]
                    target[low, p, r : r + 8, :] = base + shifted(source, high, p, r, to_low)
                    target[high, p, r : r + 8, :] = base + shifted(source, high, p, r, to_high)
                return carry

            lax.fori_loop(0, 4, step, 0)
        clear(target)
        source, target = target, source

    level = LEVELS - 1
    span = 1 << level
    last_moves = [(moves(level, low), moves(level, low + span)) for low in range(span)]
    for t in range(2):
        for r in range(BASE, BASE + ROWS, 8):
            values = []
            for low in range(span):
                high = low + span
                for move in last_moves[low]:
                    psi = source[low, t, r : r + 8, :] + shifted(source, high, t, r, move)
                    phi = source[low, 2 + t, r : r + 8, :] + shifted(source, high, 2 + t, r, move)
                    values.append(psi * lax.rsqrt(phi))
            peak = values[0]
            for value in values[1:]:
                peak = jnp.maximum(peak, value)
            total = jnp.exp(values[0] - peak)
            for value in values[1:]:
                total = total + jnp.exp(value - peak)
            out_ref[r - BASE : r - BASE + 8, t * LANES : (t + 1) * LANES] = peak + jnp.log(total)


def smem():
    return pl.BlockSpec(memory_space=pltpu.SMEM)


def vmem():
    return pl.BlockSpec(memory_space=pltpu.VMEM)


def limits():
    return pltpu.CompilerParams(vmem_limit_bytes=48 * 1024 * 1024)


def on_device(image, inv_variance, psf_rows, psf_cols, shift_num):
    sky_count = lax.axis_size("sky")
    where = jnp.stack([lax.axis_index("epoch"), lax.axis_index("sky"), sky_count]).astype(jnp.int32)
    packed = pl.pallas_call(
        pack_kernel,
        out_shape=jax.ShapeDtypeStruct((PEERS, SEND_ROWS, LANES), BF16),
        in_specs=[smem(), vmem(), vmem()],
        out_specs=vmem(),
        compiler_params=limits(),
        name="pack",
    )(where, image, inv_variance)
    got = lax.all_to_all(packed, "epoch", 0, 0, tiled=True)
    halo_shape = jax.ShapeDtypeStruct((HALO_SEND, LANES), BF16)
    near, far = pl.pallas_call(
        halo_kernel,
        out_shape=(halo_shape, halo_shape),
        in_specs=[smem(), vmem()],
        out_specs=(vmem(), vmem()),
        scratch_shapes=[
            pltpu.VMEM((PEERS + 1, EDGE_ROW, LANES), F32),
            pltpu.VMEM((HALO_SEND, LANES), F32),
            pltpu.VMEM((HALO_SEND, LANES), F32),
        ],
        compiler_params=limits(),
        name="halo",
    )(where, got)
    far = lax.ppermute(far, "sky", [(i, i + 1) if i % 2 else (i, i - 1) for i in range(1, sky_count - 1)])
    near = lax.ppermute(near, "sky", [(i, i ^ 1) for i in range(sky_count)])
    own, taps = pl.pallas_call(
        own_kernel,
        out_shape=(
            jax.ShapeDtypeStruct((EPOCHS, 4, ROWS, LANES), F32),
            jax.ShapeDtypeStruct((4, COLS + LANES, COLS), BF16),
        ),
        in_specs=[smem(), vmem()],
        out_specs=(vmem(), vmem()),
        scratch_shapes=[pltpu.VMEM((EPOCHS * ROWS, COLS + LANES), F32)] * 2,
        compiler_params=limits(),
        cost_estimate=pl.CostEstimate(flops=1_000_000_000, bytes_accessed=8_000_000, transcendentals=0),
        name="own",
    )(psf_cols, got)
    return pl.pallas_call(
        stack_kernel,
        out_shape=jax.ShapeDtypeStruct((ROWS, COLS), F32),
        in_specs=[smem(), smem(), smem(), vmem(), vmem(), vmem(), vmem()],
        out_specs=vmem(),
        scratch_shapes=[
            pltpu.VMEM((2, HALO_SEND, LANES), F32),
            pltpu.VMEM((2 * HALO_ROWS, COLS + LANES), F32),
            pltpu.VMEM((2 * HALO_ROWS, COLS + LANES), F32),
            pltpu.VMEM((4, 2 * HALO_ROWS, LANES), F32),
            pltpu.VMEM((EPOCHS, 4, SPAN, LANES), F32),
            pltpu.VMEM((EPOCHS, 4, SPAN, LANES), F32),
            pltpu.VMEM((EPOCHS, 4, SPAN, LANES), F32),
        ],
        compiler_params=limits(),
        cost_estimate=pl.CostEstimate(flops=1_000_000_000, bytes_accessed=8_000_000, transcendentals=400_000),
        name="stack",
    )(where, psf_rows, shift_num, own, taps, near, far)


def solution(mesh):
    return jax.shard_map(
        on_device,
        mesh=mesh,
        in_specs=(P("epoch", "sky", None), P("epoch", "sky", None), P(), P(), P()),
        out_specs=P("sky", "epoch"),
        check_vma=False,
    )
```

```python
import functools

import jax
import jax.numpy as jnp
from jax import lax
from jax.experimental import pallas as pl
from jax.experimental.pallas import tpu as pltpu
from jax.sharding import PartitionSpec as P

EPOCHS = 16
LEVELS = 4
PSF = 9
REACH = 4
PEERS = 8
ROWS = 48
LANES = 128
COLS = 256
EDGE_ROW = 8 * ROWS
SEND_ROWS = 9 * ROWS
HALO = [2 * j + REACH for j in range(EPOCHS)]
HALO_AT = [sum(HALO[:j]) for j in range(EPOCHS)]
HALO_ROWS = sum(HALO)
EDGE_LO = HALO[7]
EDGE_HI = HALO[15]
EDGE_LO_AT = 4 * HALO_ROWS
EDGE_HI_AT = EDGE_LO_AT + EDGE_LO
HALO_SEND = 1280
BASE = 40
SPAN = 128
F32 = jnp.float32
BF16 = jnp.bfloat16


def edge_lane(array, j):
    return 32 * ((j // 2) % 4) + (2 * array + j % 2) * 8


def pack_kernel(image_hbm, variance_hbm, out_hbm, held, blocks, sums, edges, arrived, sent):
    turn = 32 * (lax.axis_index("epoch") % 4)
    lane = lax.broadcasted_iota(jnp.int32, (ROWS, LANES), 1)
    copies = []
    for a, ref in enumerate((image_hbm, variance_hbm)):
        for i in range(2):
            copies.append(pltpu.make_async_copy(ref.at[i], held.at[2 * a + i], arrived.at[2 * a + i]))
            copies[-1].start()

    def edge(b, c):
        picked = jnp.zeros((ROWS, LANES), F32)
        if c > 0:
            left = held[b, :, (2 * c - 1) * LANES : 2 * c * LANES].astype(F32)
            picked = jnp.where(lane >= LANES - REACH, left, picked)
        if c < PEERS - 1:
            right = held[b, :, (2 * c + 2) * LANES : (2 * c + 3) * LANES].astype(F32)
            picked = jnp.where(lane < REACH, right, picked)
        return pltpu.roll(picked, b * 8 + REACH, 1)

    out = []

    def send(source, n, row, height):
        out.append(pltpu.make_async_copy(source, out_hbm.at[:, pl.ds(row, height), :], sent.at[n]))
        out[-1].start()

    for b in range(4):
        copies[b].wait()
        for c in range(PEERS):
            for t in range(2):
                lanes = slice((2 * c + t) * LANES, (2 * c + t + 1) * LANES)
                blocks[b, c, t * ROWS : (t + 1) * ROWS, :] = held[b, :, lanes]
        send(blocks.at[b], b, 2 * b * ROWS, 2 * ROWS)
        for c in range(PEERS):
            total = edge(b, c)
            if b > 0:
                total = total + sums[c]
            if b < 3:
                sums[c] = total
            else:
                edges[c] = pltpu.roll(total, turn, 1).astype(BF16)
    send(edges, 4, EDGE_ROW, ROWS)
    for copy in out:
        copy.wait()


def build_halo(to_far, got_ref, out_ref, wide, out):
    core = lax.axis_index("sky") % 2
    last = core if to_far else 1 - core

    def take(index, source_row, target_row, height):
        start = source_row + last * (ROWS - height)
        out[target_row : target_row + height, :] = wide[index, pl.ds(start, height), :]

    for k in range(PEERS):
        wide[k] = got_ref[k, :EDGE_ROW, :].astype(F32)
    for half in range(2):
        total = got_ref[4 * half, EDGE_ROW:SEND_ROWS, :].astype(F32)
        for k in range(4 * half + 1, 4 * half + 4):
            total = total + got_ref[k, EDGE_ROW:SEND_ROWS, :].astype(F32)
        wide[PEERS, half * ROWS : (half + 1) * ROWS, :] = total
    for j in range(EPOCHS):
        for a in range(2):
            for t in range(2):
                row = ((a * 2 + j % 2) * 2 + t) * ROWS
                take(j // 2, row, (a * 2 + t) * HALO_ROWS + HALO_AT[j], HALO[j])
    take(PEERS, 0, EDGE_LO_AT, EDGE_LO)
    take(PEERS, ROWS, EDGE_HI_AT, EDGE_HI)
    rest = EDGE_HI_AT + EDGE_HI
    out[rest:HALO_SEND, :] = jnp.zeros((HALO_SEND - rest, LANES), F32)
    out_ref[...] = out[...].astype(BF16)


def split(values):
    high = values.astype(BF16)
    return high, (values - high.astype(F32)).astype(BF16)


def column_filter(image, variance, taps):
    high, low = split(image * variance)
    variance = variance.astype(BF16)

    def dot(left, right):
        return jnp.dot(left, right, preferred_element_type=F32)

    psi = dot(high, taps[0]) + (dot(low, taps[0]) + dot(high, taps[1]))
    phi = dot(variance, taps[2]) + dot(variance, taps[3])
    return psi, phi


def own_kernel(cols_ref, got_ref, out_ref, taps_ref, image, variance):
    shape = (COLS + LANES, COLS)
    place = lax.broadcasted_iota(jnp.int32, shape, 0)
    place = jnp.where(place < COLS + LANES // 2, place, place - (COLS + LANES))
    step = place - lax.broadcasted_iota(jnp.int32, shape, 1) + REACH
    psi_taps = jnp.zeros(shape, F32)
    phi_taps = jnp.zeros(shape, F32)
    for b in range(PSF):
        hit = step == b
        psi_taps = jnp.where(hit, cols_ref[b], psi_taps)
        phi_taps = jnp.where(hit, cols_ref[b] * cols_ref[b], phi_taps)
    taps_ref[0], taps_ref[1] = split(psi_taps)
    taps_ref[2], taps_ref[3] = split(phi_taps)
    edges = []
    for half in range(2):
        total = got_ref[4 * half, EDGE_ROW:SEND_ROWS, :].astype(F32)
        for k in range(4 * half + 1, 4 * half + 4):
            total = total + got_ref[k, EDGE_ROW:SEND_ROWS, :].astype(F32)
        edges.append(total)
    for j in range(EPOCHS):
        for a, ref in enumerate((image, variance)):
            for t in range(2):
                row = ((a * 2 + j % 2) * 2 + t) * ROWS
                ref[j * ROWS : (j + 1) * ROWS, t * LANES : (t + 1) * LANES] = got_ref[
                    j // 2, row : row + ROWS, :
                ].astype(F32)
            turn = (LANES - REACH - edge_lane(a, j)) % LANES
            ref[j * ROWS : (j + 1) * ROWS, COLS:] = pltpu.roll(edges[j // 8], turn, 1)
    psi, phi = column_filter(image[...], variance[...], taps_ref)
    for j in range(EPOCHS):
        rows = slice(j * ROWS, (j + 1) * ROWS)
        for t in range(2):
            lanes = slice(t * LANES, (t + 1) * LANES)
            out_ref[j, t] = psi[rows, lanes]
            out_ref[j, 2 + t] = phi[rows, lanes]


def put_halo(above, wide, taps_ref, image, variance, filtered, maps):
    for a, ref in enumerate((image, variance)):
        for t in range(2):
            start = (a * 2 + t) * HALO_ROWS
            ref[:, t * LANES : (t + 1) * LANES] = wide[start : start + HALO_ROWS, :]
        for j in range(EPOCHS):
            start, height = (EDGE_LO_AT, EDGE_LO) if j < 8 else (EDGE_HI_AT, EDGE_HI)
            start = start + above * (height - HALO[j])
            turn = (LANES - REACH - edge_lane(a, j)) % LANES
            ref[HALO_AT[j] : HALO_AT[j] + HALO[j], COLS:] = pltpu.roll(wide[pl.ds(start, HALO[j]), :], turn, 1)
    psi, phi = column_filter(image[...], variance[...], taps_ref)
    for t in range(2):
        lanes = slice(t * LANES, (t + 1) * LANES)
        filtered[t] = psi[:, lanes]
        filtered[2 + t] = phi[:, lanes]
    for j in range(EPOCHS):
        start = jnp.where(above == 1, BASE - HALO[j], BASE + ROWS)
        for p in range(4):
            maps[j, p, pl.ds(start, HALO[j]), :] = filtered[p, HALO_AT[j] : HALO_AT[j] + HALO[j], :]


def slot(level, j):
    done = j & ((1 << level) - 1)
    if not done:
        return j
    b = done.bit_length() - 1
    return EPOCHS + 8 * b + ((j >> (b + 1)) << b | (j & ((1 << b) - 1)))


def moves(shift_ref, level, j):
    number = shift_ref[level, j]
    whole = lax.shift_right_arithmetic(number, 2)
    part = number - whole * 4
    fraction = part.astype(F32) * 0.25
    behind = jnp.where(part > 0, whole + 1, whole)
    return whole, behind, 1.0 - fraction, fraction


def shifted(ref, place, p, r, height, move):
    whole, behind, keep, fraction = move
    return keep * ref[place, p, pl.ds(r - whole, height), :] + fraction * ref[place, p, pl.ds(r - behind, height), :]


EDGE = [REACH, REACH + 2, REACH + 6, REACH + 14]


def span_of(core, level, reach, far):
    height = EDGE[level] + reach if far else ROWS - EDGE[level] + reach
    count = -(-height // 8)
    top, bottom = BASE + EDGE[level], BASE + ROWS - EDGE[level]
    if far:
        return jnp.where(core == 0, top - 8 * count, bottom), count
    return jnp.where(core == 0, top, bottom - 8 * count), count


def filter_rows(core, far, rows_ref, maps, stacks):
    taps = [[rows_ref[a] for a in range(PSF)], [rows_ref[a] * rows_ref[a] for a in range(PSF)]]
    for j in range(EPOCHS):
        start, count = span_of(core, 0, 2 * j, far)
        for m in range(2):

            def one(t, carry, j=j, m=m, start=start, count=count):
                p = 2 * m + t
                total = taps[m][0] * maps[j, p, pl.ds(start - REACH, 8 * count), :]
                for a in range(1, PSF):
                    total = total + taps[m][a] * maps[j, p, pl.ds(start - REACH + a, 8 * count), :]
                stacks[j, p, pl.ds(start, 8 * count), :] = total
                return carry

            lax.fori_loop(0, 2, one, 0)


BATCH = 12


def run_level(core, far, level, shift_ref, stacks):
    held, size = [], 0

    def store():
        for place, p, rows, value in held:
            stacks[place, p, rows, :] = value
        held.clear()

    for low in range(EPOCHS):
        if low >> level & 1:
            continue
        high = low + (1 << level)
        reach = 2 * (low >> (level + 1) << (level + 1))
        start, count = span_of(core, level + 1, reach, far)
        rows = pl.ds(start, 8 * count)
        to_low, to_high = moves(shift_ref, level, low), moves(shift_ref, level, high)
        from_at = slot(level, high)
        for p in range(4):
            if size + count > BATCH:
                store()
                size = 0
            base = stacks[slot(level, low), p, rows, :]
            for place, move in ((slot(level + 1, low), to_low), (slot(level + 1, high), to_high)):
                held.append((place, p, rows, base + shifted(stacks, from_at, p, start, 8 * count, move)))
            size += count
    store()


def inner_kernel(
    rows_ref, shift_ref, own_ref, taps_ref, near_ref, stacks, wide, image, variance, filtered, maps
):
    core = lax.axis_index("sky") % 2
    wide[...] = near_ref[...].astype(F32)
    put_halo(core, wide, taps_ref, image, variance, filtered, maps)
    for j in range(EPOCHS):
        for p in range(4):
            maps[j, p, BASE : BASE + ROWS, :] = own_ref[j, p]
    filter_rows(core, False, rows_ref, maps, stacks)
    for level in range(LEVELS - 1):
        run_level(core, False, level, shift_ref, stacks)


def outer_kernel(
    rows_ref,
    shift_ref,
    own_ref,
    taps_ref,
    far_ref,
    stacks_in,
    out_ref,
    stacks,
    wide,
    image,
    variance,
    filtered,
    maps,
    values,
):
    sky = lax.axis_index("sky")
    sky_last = lax.axis_size("sky") - 1
    core = sky % 2

    def clear(level):
        @pl.when(sky == 0)
        def _():
            for j in range(EPOCHS):
                stacks[slot(level, j), :, :BASE, :] = jnp.zeros((4, BASE, LANES), F32)

        @pl.when(sky == sky_last)
        def _():
            for j in range(EPOCHS):
                stacks[slot(level, j), :, BASE + ROWS :, :] = jnp.zeros((4, SPAN - BASE - ROWS, LANES), F32)

    wide[...] = far_ref[...].astype(F32)
    put_halo(1 - core, wide, taps_ref, image, variance, filtered, maps)
    own_rows = core * (ROWS - 8)
    for j in range(EPOCHS):
        for p in range(4):
            maps[j, p, pl.ds(BASE + own_rows, 8), :] = own_ref[j, p, pl.ds(own_rows, 8), :]
    filter_rows(core, True, rows_ref, maps, stacks)
    clear(0)
    for level in range(LEVELS - 1):
        run_level(core, True, level, shift_ref, stacks)
        clear(level + 1)
    level = LEVELS - 1
    half = 1 << level
    last_moves = [(moves(shift_ref, level, low), moves(shift_ref, level, low + half)) for low in range(half)]
    for t in range(2):
        peak = None
        for low in range(half):
            base_at, from_at = slot(level, low), slot(level, low + half)
            psi_base = stacks[base_at, t, BASE : BASE + ROWS, :]
            phi_base = stacks[base_at, 2 + t, BASE : BASE + ROWS, :]
            for side, move in enumerate(last_moves[low]):
                psi = psi_base + shifted(stacks, from_at, t, BASE, ROWS, move)
                phi = phi_base + shifted(stacks, from_at, 2 + t, BASE, ROWS, move)
                value = psi * lax.rsqrt(phi)
                values[low + side * half] = value
                peak = value if peak is None else jnp.maximum(peak, value)
        total = jnp.exp(values[0] - peak)
        for v in range(1, EPOCHS):
            total = total + jnp.exp(values[v] - peak)
        out_ref[:, t * LANES : (t + 1) * LANES] = peak + jnp.log(total)


SLOTS = EPOCHS + 8 * (LEVELS - 1)


def smem():
    return pl.BlockSpec(memory_space=pltpu.SMEM)


def vmem():
    return pl.BlockSpec(memory_space=pltpu.VMEM)


def limits(mebibytes=32):
    return pltpu.CompilerParams(vmem_limit_bytes=mebibytes * 1024 * 1024)


def cost(microseconds):
    return pl.CostEstimate(flops=microseconds * 1_000_000_000, bytes_accessed=microseconds * 3_000_000, transcendentals=0)


def send_halo(to_far, got, name):
    return pl.pallas_call(
        functools.partial(build_halo, to_far),
        out_shape=jax.ShapeDtypeStruct((HALO_SEND, LANES), BF16),
        in_specs=[vmem()],
        out_specs=vmem(),
        scratch_shapes=[pltpu.VMEM((PEERS + 1, EDGE_ROW, LANES), F32), pltpu.VMEM((HALO_SEND, LANES), F32)],
        compiler_params=limits(),
        cost_estimate=cost(1),
        name=name,
    )(got)


def on_device(image, inv_variance, psf_rows, psf_cols, shift_num):
    sky_count = lax.axis_size("sky")
    cols = image.shape[2]
    packed = pl.pallas_call(
        pack_kernel,
        out_shape=jax.ShapeDtypeStruct((PEERS, SEND_ROWS, LANES), BF16),
        in_specs=[pl.BlockSpec(memory_space=pltpu.HBM), pl.BlockSpec(memory_space=pltpu.HBM)],
        out_specs=pl.BlockSpec(memory_space=pltpu.HBM),
        scratch_shapes=[
            pltpu.VMEM((4, ROWS, cols), BF16),
            pltpu.VMEM((4, PEERS, 2 * ROWS, LANES), BF16),
            pltpu.VMEM((PEERS, ROWS, LANES), F32),
            pltpu.VMEM((PEERS, ROWS, LANES), BF16),
            pltpu.SemaphoreType.DMA((4,)),
            pltpu.SemaphoreType.DMA((5,)),
        ],
        compiler_params=limits(60),
        cost_estimate=cost(2),
        name="pack",
    )(image, inv_variance)
    got = lax.all_to_all(packed, "epoch", 0, 0, tiled=True)
    near = send_halo(False, got, "near")
    near = lax.ppermute(near, "sky", [(i, i ^ 1) for i in range(sky_count)])
    far = send_halo(True, got, "far")
    far = lax.ppermute(far, "sky", [(i, i + 1) if i % 2 else (i, i - 1) for i in range(1, sky_count - 1)])
    own, taps = pl.pallas_call(
        own_kernel,
        out_shape=(
            jax.ShapeDtypeStruct((EPOCHS, 4, ROWS, LANES), F32),
            jax.ShapeDtypeStruct((4, COLS + LANES, COLS), BF16),
        ),
        in_specs=[smem(), vmem()],
        out_specs=(vmem(), vmem()),
        scratch_shapes=[pltpu.VMEM((EPOCHS * ROWS, COLS + LANES), F32)] * 2,
        compiler_params=limits(),
        cost_estimate=cost(5),
        name="own",
    )(psf_cols, got)
    stacks_shape = jax.ShapeDtypeStruct((SLOTS, 4, SPAN, LANES), F32)
    work = [
        pltpu.VMEM((HALO_SEND, LANES), F32),
        pltpu.VMEM((HALO_ROWS, COLS + LANES), F32),
        pltpu.VMEM((HALO_ROWS, COLS + LANES), F32),
        pltpu.VMEM((4, HALO_ROWS, LANES), F32),
        pltpu.VMEM((EPOCHS, 4, SPAN, LANES), F32),
    ]
    stacks = pl.pallas_call(
        inner_kernel,
        out_shape=stacks_shape,
        in_specs=[smem(), smem(), vmem(), vmem(), vmem()],
        out_specs=vmem(),
        scratch_shapes=work,
        compiler_params=limits(),
        cost_estimate=cost(5),
        name="inner",
    )(psf_rows, shift_num, own, taps, near)
    out, _ = pl.pallas_call(
        outer_kernel,
        out_shape=(jax.ShapeDtypeStruct((ROWS, COLS), F32), stacks_shape),
        in_specs=[smem(), smem(), vmem(), vmem(), vmem(), vmem()],
        out_specs=(vmem(), vmem()),
        scratch_shapes=[*work, pltpu.VMEM((EPOCHS, ROWS, LANES), F32)],
        input_output_aliases={5: 1},
        compiler_params=limits(),
        cost_estimate=cost(5),
        name="outer",
    )(psf_rows, shift_num, own, taps, far, stacks)
    return out


def solution(mesh):
    return jax.shard_map(
        on_device,
        mesh=mesh,
        in_specs=(P("epoch", "sky", None), P("epoch", "sky", None), P(), P(), P()),
        out_specs=P("sky", "epoch"),
        check_vma=False,
    )
```

```python
import functools

import jax
import jax.numpy as jnp
from jax import lax
from jax.experimental import pallas as pl
from jax.experimental.pallas import tpu as pltpu
from jax.sharding import PartitionSpec as P

EPOCHS = 16
LEVELS = 4
PSF = 9
REACH = 4
PEERS = 8
ROWS = 48
LANES = 128
COLS = 256
EDGE_ROW = 8 * ROWS
PIECE = 16
SEND_ROWS = EDGE_ROW + PIECE
HALO = [2 * j + REACH for j in range(EPOCHS)]
HALO_AT = [sum(HALO[:j]) for j in range(EPOCHS)]
HALO_ROWS = sum(HALO)
EDGE_LO = HALO[7]
EDGE_HI = HALO[15]
EDGE_LO_AT = 4 * HALO_ROWS
EDGE_HI_AT = EDGE_LO_AT + EDGE_LO
HALO_SEND = 1280
BASE = 40
SPAN = 128
F32 = jnp.float32
BF16 = jnp.bfloat16


def edge_lane(array, j):
    return 32 * ((j // 2) % 4) + (2 * array + j % 2) * 8


def pack_kernel(image_hbm, variance_hbm, out_hbm, held, blocks, sums, edges, arrived, sent):
    lane = lax.broadcasted_iota(jnp.int32, (ROWS, LANES), 1)
    copies = []
    for a, ref in enumerate((image_hbm, variance_hbm)):
        for i in range(2):
            copies.append(pltpu.make_async_copy(ref.at[i], held.at[2 * a + i], arrived.at[2 * a + i]))
            copies[-1].start()

    def edge(b, c):
        picked = jnp.zeros((ROWS, LANES), F32)
        if c > 0:
            left = held[b, :, (2 * c - 1) * LANES : 2 * c * LANES].astype(F32)
            picked = jnp.where(lane >= LANES - REACH, left, picked)
        if c < PEERS - 1:
            right = held[b, :, (2 * c + 2) * LANES : (2 * c + 3) * LANES].astype(F32)
            picked = jnp.where(lane < REACH, right, picked)
        return pltpu.roll(picked, b * 8 + REACH, 1)

    out = []

    def send(source, n, row, height):
        out.append(pltpu.make_async_copy(source, out_hbm.at[:, pl.ds(row, height), :], sent.at[n]))
        out[-1].start()

    for b in range(4):
        copies[b].wait()
        for c in range(PEERS):
            for t in range(2):
                lanes = slice((2 * c + t) * LANES, (2 * c + t + 1) * LANES)
                blocks[b, c, t * ROWS : (t + 1) * ROWS, :] = held[b, :, lanes]
        send(blocks.at[b], b, 2 * b * ROWS, 2 * ROWS)
        for c in range(PEERS):
            total = edge(b, c)
            if b > 0:
                total = total + sums[c]
            if b < 3:
                sums[c] = total
            else:
                pieces = total[:PIECE]
                for g in range(1, ROWS // PIECE):
                    pieces = pieces + pltpu.roll(total[g * PIECE : (g + 1) * PIECE], 32 * g, 1)
                edges[c] = pieces.astype(BF16)
    send(edges, 4, EDGE_ROW, PIECE)
    for copy in out:
        copy.wait()


def gather_edges(got_ref, edges_ref):
    owner = lax.broadcasted_iota(jnp.int32, (PIECE, LANES), 1) // 32
    pieces = [got_ref[k, EDGE_ROW:SEND_ROWS, :].astype(F32) for k in range(PEERS)]
    for half in range(2):
        for g in range(ROWS // PIECE):
            total = jnp.zeros((PIECE, LANES), F32)
            for k in range(4):
                turn = 32 * ((k - g) % 4)
                piece = pieces[4 * half + k]
                total = jnp.where(owner == k, pltpu.roll(piece, turn, 1) if turn else piece, total)
            edges_ref[half * ROWS + g * PIECE : half * ROWS + (g + 1) * PIECE, :] = total


def build_halo(to_far, got_ref, edges_ref, out_ref, wide, out):
    core = lax.axis_index("sky") % 2
    last = core if to_far else 1 - core
    for k in range(PEERS):
        wide[k] = got_ref[k, :EDGE_ROW, :].astype(F32)
    for j in range(EPOCHS):
        for a in range(2):
            for t in range(2):
                source = ((a * 2 + j % 2) * 2 + t) * ROWS + last * (ROWS - HALO[j])
                row = (a * 2 + t) * HALO_ROWS + HALO_AT[j]
                out[row : row + HALO[j], :] = wide[j // 2, pl.ds(source, HALO[j]), :]
    out[EDGE_LO_AT:EDGE_HI_AT, :] = edges_ref[pl.ds(last * (ROWS - EDGE_LO), EDGE_LO), :]
    rest = EDGE_HI_AT + EDGE_HI
    out[EDGE_HI_AT:rest, :] = edges_ref[pl.ds(ROWS + last * (ROWS - EDGE_HI), EDGE_HI), :]
    out[rest:HALO_SEND, :] = jnp.zeros((HALO_SEND - rest, LANES), F32)
    out_ref[...] = out[...].astype(BF16)


def halo_kernel(to_far, got_ref, out_ref, edges_ref, wide, out):
    gather_edges(got_ref, edges_ref)
    build_halo(to_far, got_ref, edges_ref, out_ref, wide, out)


def split(values):
    high = values.astype(BF16)
    return high, (values - high.astype(F32)).astype(BF16)


def column_filter(image, variance, taps):
    high, low = split(image.astype(F32) * variance.astype(F32))

    def dot(left, right):
        return jnp.dot(left, right, preferred_element_type=F32)

    psi = dot(high, taps[0]) + (dot(low, taps[0]) + dot(high, taps[1]))
    phi = dot(variance, taps[2]) + dot(variance, taps[3])
    return psi, phi


def own_kernel(cols_ref, got_ref, edges_ref, out_ref, taps_ref, image, variance):
    shape = (COLS + LANES, COLS)
    place = lax.broadcasted_iota(jnp.int32, shape, 0)
    place = jnp.where(place < COLS + LANES // 2, place, place - (COLS + LANES))
    step = place - lax.broadcasted_iota(jnp.int32, shape, 1) + REACH
    psi_taps = jnp.zeros(shape, F32)
    phi_taps = jnp.zeros(shape, F32)
    for b in range(PSF):
        hit = step == b
        psi_taps = jnp.where(hit, cols_ref[b], psi_taps)
        phi_taps = jnp.where(hit, cols_ref[b] * cols_ref[b], phi_taps)
    taps_ref[0], taps_ref[1] = split(psi_taps)
    taps_ref[2], taps_ref[3] = split(phi_taps)
    for j in range(EPOCHS):
        for a, ref in enumerate((image, variance)):
            for t in range(2):
                row = ((a * 2 + j % 2) * 2 + t) * ROWS
                ref[j * ROWS : (j + 1) * ROWS, t * LANES : (t + 1) * LANES] = got_ref[
                    j // 2, row : row + ROWS, :
                ].astype(F32)
            turn = (LANES - REACH - edge_lane(a, j)) % LANES
            ref[j * ROWS : (j + 1) * ROWS, COLS:] = pltpu.roll(edges_ref[j // 8 * ROWS : (j // 8 + 1) * ROWS, :], turn, 1)
    psi, phi = column_filter(image[...].astype(BF16), variance[...].astype(BF16), taps_ref)
    for j in range(EPOCHS):
        rows = slice(j * ROWS, (j + 1) * ROWS)
        for t in range(2):
            lanes = slice(t * LANES, (t + 1) * LANES)
            out_ref[j, t] = psi[rows, lanes]
            out_ref[j, 2 + t] = phi[rows, lanes]


def put_halo(above, halo_ref, taps_ref, edges, filtered, maps):
    edges[0, : HALO_SEND - EDGE_LO_AT, :] = halo_ref[EDGE_LO_AT:HALO_SEND, :].astype(F32)
    for a in range(2):
        for j in range(EPOCHS):
            start, height = (0, EDGE_LO) if j < 8 else (EDGE_LO, EDGE_HI)
            start = start + above * (height - HALO[j])
            turn = (LANES - REACH - edge_lane(a, j)) % LANES
            piece = edges[0, pl.ds(start, HALO[j]), :]
            edges[1 + a, HALO_AT[j] : HALO_AT[j] + HALO[j], :] = pltpu.roll(piece, turn, 1)

    def extended(a):
        left = halo_ref[2 * a * HALO_ROWS : (2 * a + 1) * HALO_ROWS, :]
        right = halo_ref[(2 * a + 1) * HALO_ROWS : (2 * a + 2) * HALO_ROWS, :]
        return jnp.concatenate([left, right, edges[1 + a].astype(BF16)], axis=1)

    psi, phi = column_filter(extended(0), extended(1), taps_ref)
    for t in range(2):
        lanes = slice(t * LANES, (t + 1) * LANES)
        filtered[t] = psi[:, lanes]
        filtered[2 + t] = phi[:, lanes]
    for j in range(EPOCHS):
        start = jnp.where(above == 1, BASE - HALO[j], BASE + ROWS)
        for p in range(4):
            maps[j, p, pl.ds(start, HALO[j]), :] = filtered[p, HALO_AT[j] : HALO_AT[j] + HALO[j], :]


def slot(level, j):
    done = j & ((1 << level) - 1)
    if not done:
        return j
    b = done.bit_length() - 1
    return EPOCHS + 8 * b + ((j >> (b + 1)) << b | (j & ((1 << b) - 1)))


def moves(shift_ref, level, j):
    number = shift_ref[level, j]
    whole = lax.shift_right_arithmetic(number, 2)
    part = number - whole * 4
    fraction = part.astype(F32) * 0.25
    behind = jnp.where(part > 0, whole + 1, whole)
    return whole, behind, 1.0 - fraction, fraction


def shifted(ref, place, p, r, height, move):
    whole, behind, keep, fraction = move
    return keep * ref[place, p, pl.ds(r - whole, height), :] + fraction * ref[place, p, pl.ds(r - behind, height), :]


EDGE = [REACH, REACH + 2, REACH + 6, REACH + 14]


def span_of(core, level, reach, far):
    height = EDGE[level] + reach if far else ROWS - EDGE[level] + reach
    count = -(-height // 8)
    top, bottom = BASE + EDGE[level], BASE + ROWS - EDGE[level]
    if far:
        return jnp.where(core == 0, top - 8 * count, bottom), count
    return jnp.where(core == 0, top, bottom - 8 * count), count


def filter_rows(core, far, rows_ref, maps, stacks):
    taps = [[rows_ref[a] for a in range(PSF)], [rows_ref[a] * rows_ref[a] for a in range(PSF)]]
    for j in range(EPOCHS):
        start, count = span_of(core, 0, 2 * j, far)
        for p in range(4):
            factors = taps[p // 2]
            total = factors[0] * maps[j, p, pl.ds(start - REACH, 8 * count), :]
            for a in range(1, PSF):
                total = total + factors[a] * maps[j, p, pl.ds(start - REACH + a, 8 * count), :]
            stacks[j, p, pl.ds(start, 8 * count), :] = total


BATCH = 12


def run_level(core, far, level, shift_ref, stacks):
    held, size = [], 0

    def store():
        for place, p, rows, value in held:
            stacks[place, p, rows, :] = value
        held.clear()

    for low in range(EPOCHS):
        if low >> level & 1:
            continue
        high = low + (1 << level)
        reach = 2 * (low >> (level + 1) << (level + 1))
        start, count = span_of(core, level + 1, reach, far)
        rows = pl.ds(start, 8 * count)
        to_low, to_high = moves(shift_ref, level, low), moves(shift_ref, level, high)
        from_at = slot(level, high)
        for p in range(4):
            if size + count > BATCH:
                store()
                size = 0
            base = stacks[slot(level, low), p, rows, :]
            for place, move in ((slot(level + 1, low), to_low), (slot(level + 1, high), to_high)):
                held.append((place, p, rows, base + shifted(stacks, from_at, p, start, 8 * count, move)))
            size += count
    store()


def inner_kernel(
    rows_ref, shift_ref, own_ref, taps_ref, near_ref, stacks, edges, filtered, maps
):
    core = lax.axis_index("sky") % 2
    put_halo(core, near_ref, taps_ref, edges, filtered, maps)
    for j in range(EPOCHS):
        for p in range(4):
            maps[j, p, BASE : BASE + ROWS, :] = own_ref[j, p]
    filter_rows(core, False, rows_ref, maps, stacks)
    for level in range(LEVELS - 1):
        run_level(core, False, level, shift_ref, stacks)


def outer_kernel(
    rows_ref,
    shift_ref,
    own_ref,
    taps_ref,
    far_ref,
    stacks_in,
    out_ref,
    stacks,
    edges,
    filtered,
    maps,
    values,
):
    sky = lax.axis_index("sky")
    sky_last = lax.axis_size("sky") - 1
    core = sky % 2

    def clear(level):
        @pl.when(sky == 0)
        def _():
            for j in range(EPOCHS):
                stacks[slot(level, j), :, :BASE, :] = jnp.zeros((4, BASE, LANES), F32)

        @pl.when(sky == sky_last)
        def _():
            for j in range(EPOCHS):
                stacks[slot(level, j), :, BASE + ROWS :, :] = jnp.zeros((4, SPAN - BASE - ROWS, LANES), F32)

    put_halo(1 - core, far_ref, taps_ref, edges, filtered, maps)
    own_rows = core * (ROWS - 8)
    for j in range(EPOCHS):
        for p in range(4):
            maps[j, p, pl.ds(BASE + own_rows, 8), :] = own_ref[j, p, pl.ds(own_rows, 8), :]
    filter_rows(core, True, rows_ref, maps, stacks)
    clear(0)
    for level in range(LEVELS - 1):
        run_level(core, True, level, shift_ref, stacks)
        clear(level + 1)
    level = LEVELS - 1
    half = 1 << level
    last_moves = [(moves(shift_ref, level, low), moves(shift_ref, level, low + half)) for low in range(half)]
    for t in range(2):
        peak = None
        for low in range(half):
            base_at, from_at = slot(level, low), slot(level, low + half)
            psi_base = stacks[base_at, t, BASE : BASE + ROWS, :]
            phi_base = stacks[base_at, 2 + t, BASE : BASE + ROWS, :]
            for side, move in enumerate(last_moves[low]):
                psi = psi_base + shifted(stacks, from_at, t, BASE, ROWS, move)
                phi = phi_base + shifted(stacks, from_at, 2 + t, BASE, ROWS, move)
                value = psi * lax.rsqrt(phi)
                values[low + side * half] = value
                peak = value if peak is None else jnp.maximum(peak, value)
        total = jnp.exp(values[0] - peak)
        for v in range(1, EPOCHS):
            total = total + jnp.exp(values[v] - peak)
        out_ref[:, t * LANES : (t + 1) * LANES] = peak + jnp.log(total)


SLOTS = EPOCHS + 8 * (LEVELS - 1)


def smem():
    return pl.BlockSpec(memory_space=pltpu.SMEM)


def vmem():
    return pl.BlockSpec(memory_space=pltpu.VMEM)


def limits(mebibytes=32):
    return pltpu.CompilerParams(vmem_limit_bytes=mebibytes * 1024 * 1024)


def cost(microseconds):
    return pl.CostEstimate(flops=microseconds * 1_000_000_000, bytes_accessed=microseconds * 3_000_000, transcendentals=0)


def build(to_far, got, name):
    return pl.pallas_call(
        functools.partial(halo_kernel, to_far),
        out_shape=(
            jax.ShapeDtypeStruct((HALO_SEND, LANES), BF16),
            jax.ShapeDtypeStruct((2 * ROWS, LANES), F32),
        ),
        in_specs=[vmem()],
        out_specs=(vmem(), vmem()),
        scratch_shapes=[pltpu.VMEM((PEERS, EDGE_ROW, LANES), F32), pltpu.VMEM((HALO_SEND, LANES), F32)],
        compiler_params=limits(),
        cost_estimate=cost(1),
        name=name,
    )(got)


def on_device(image, inv_variance, psf_rows, psf_cols, shift_num):
    sky_count = lax.axis_size("sky")
    cols = image.shape[2]
    packed = pl.pallas_call(
        pack_kernel,
        out_shape=jax.ShapeDtypeStruct((PEERS, SEND_ROWS, LANES), BF16),
        in_specs=[pl.BlockSpec(memory_space=pltpu.HBM), pl.BlockSpec(memory_space=pltpu.HBM)],
        out_specs=pl.BlockSpec(memory_space=pltpu.HBM),
        scratch_shapes=[
            pltpu.VMEM((4, ROWS, cols), BF16),
            pltpu.VMEM((4, PEERS, 2 * ROWS, LANES), BF16),
            pltpu.VMEM((PEERS, ROWS, LANES), F32),
            pltpu.VMEM((PEERS, PIECE, LANES), BF16),
            pltpu.SemaphoreType.DMA((4,)),
            pltpu.SemaphoreType.DMA((5,)),
        ],
        compiler_params=limits(60),
        cost_estimate=cost(2),
        name="pack",
    )(image, inv_variance)
    got = lax.all_to_all(packed, "epoch", 0, 0, tiled=True)
    near, _ = build(False, got, "near")
    far, edges = build(True, got, "far")
    near = lax.ppermute(near, "sky", [(i, i ^ 1) for i in range(sky_count)])
    far = lax.ppermute(far, "sky", [(i, i + 1) if i % 2 else (i, i - 1) for i in range(1, sky_count - 1)])
    own, taps = pl.pallas_call(
        own_kernel,
        out_shape=(
            jax.ShapeDtypeStruct((EPOCHS, 4, ROWS, LANES), F32),
            jax.ShapeDtypeStruct((4, COLS + LANES, COLS), BF16),
        ),
        in_specs=[smem(), vmem(), vmem()],
        out_specs=(vmem(), vmem()),
        scratch_shapes=[pltpu.VMEM((EPOCHS * ROWS, COLS + LANES), F32)] * 2,
        compiler_params=limits(),
        cost_estimate=cost(5),
        name="own",
    )(psf_cols, got, edges)
    stacks_shape = jax.ShapeDtypeStruct((SLOTS, 4, SPAN, LANES), F32)
    work = [
        pltpu.VMEM((3, HALO_ROWS, LANES), F32),
        pltpu.VMEM((4, HALO_ROWS, LANES), F32),
        pltpu.VMEM((EPOCHS, 4, SPAN, LANES), F32),
    ]
    stacks = pl.pallas_call(
        inner_kernel,
        out_shape=stacks_shape,
        in_specs=[smem(), smem(), vmem(), vmem(), vmem()],
        out_specs=vmem(),
        scratch_shapes=work,
        compiler_params=limits(),
        cost_estimate=cost(5),
        name="inner",
    )(psf_rows, shift_num, own, taps, near)
    out, _ = pl.pallas_call(
        outer_kernel,
        out_shape=(jax.ShapeDtypeStruct((ROWS, COLS), F32), stacks_shape),
        in_specs=[smem(), smem(), vmem(), vmem(), vmem(), vmem()],
        out_specs=(vmem(), vmem()),
        scratch_shapes=[*work, pltpu.VMEM((EPOCHS, ROWS, LANES), F32)],
        input_output_aliases={5: 1},
        compiler_params=limits(),
        cost_estimate=cost(5),
        name="outer",
    )(psf_rows, shift_num, own, taps, far, stacks)
    return out


def solution(mesh):
    return jax.shard_map(
        on_device,
        mesh=mesh,
        in_specs=(P("epoch", "sky", None), P("epoch", "sky", None), P(), P(), P()),
        out_specs=P("sky", "epoch"),
        check_vma=False,
    )
```

```python
import functools

import jax
import jax.numpy as jnp
from jax import lax
from jax.experimental import pallas as pl
from jax.experimental.pallas import tpu as pltpu
from jax.sharding import PartitionSpec as P

EPOCHS = 16
LEVELS = 4
PSF = 9
REACH = 4
PEERS = 8
ROWS = 48
LANES = 128
COLS = 256
EDGE_ROW = 8 * ROWS
PIECE = 16
SEND_ROWS = EDGE_ROW + PIECE
HALO = [2 * j + REACH for j in range(EPOCHS)]
HALO_AT = [sum(HALO[:j]) for j in range(EPOCHS)]
HALO_ROWS = sum(HALO)
EDGE_LO = HALO[7]
EDGE_HI = HALO[15]
EDGE_LO_AT = 4 * HALO_ROWS
EDGE_HI_AT = EDGE_LO_AT + EDGE_LO
HALO_SEND = 1280
BASE = 40
SPAN = 128
F32 = jnp.float32
BF16 = jnp.bfloat16


def edge_lane(array, j):
    return 32 * ((j // 2) % 4) + (2 * array + j % 2) * 8


def pack_kernel(image_hbm, variance_hbm, out_hbm, held, blocks, sums, edges, arrived, sent):
    lane = lax.broadcasted_iota(jnp.int32, (ROWS, LANES), 1)
    copies = []
    for a, ref in enumerate((image_hbm, variance_hbm)):
        for i in range(2):
            copies.append(pltpu.make_async_copy(ref.at[i], held.at[2 * a + i], arrived.at[2 * a + i]))
            copies[-1].start()

    def edge(b, c):
        picked = jnp.zeros((ROWS, LANES), F32)
        if c > 0:
            left = held[b, :, (2 * c - 1) * LANES : 2 * c * LANES].astype(F32)
            picked = jnp.where(lane >= LANES - REACH, left, picked)
        if c < PEERS - 1:
            right = held[b, :, (2 * c + 2) * LANES : (2 * c + 3) * LANES].astype(F32)
            picked = jnp.where(lane < REACH, right, picked)
        return pltpu.roll(picked, b * 8 + REACH, 1)

    out = []

    def send(source, n, row, height):
        out.append(pltpu.make_async_copy(source, out_hbm.at[:, pl.ds(row, height), :], sent.at[n]))
        out[-1].start()

    for b in range(4):
        copies[b].wait()
        for c in range(PEERS):
            for t in range(2):
                lanes = slice((2 * c + t) * LANES, (2 * c + t + 1) * LANES)
                blocks[b, c, t * ROWS : (t + 1) * ROWS, :] = held[b, :, lanes]
        send(blocks.at[b], b, 2 * b * ROWS, 2 * ROWS)
        for c in range(PEERS):
            total = edge(b, c)
            if b > 0:
                total = total + sums[c]
            if b < 3:
                sums[c] = total
            else:
                pieces = total[:PIECE]
                for g in range(1, ROWS // PIECE):
                    pieces = pieces + pltpu.roll(total[g * PIECE : (g + 1) * PIECE], 32 * g, 1)
                edges[c] = pieces.astype(BF16)
    send(edges, 4, EDGE_ROW, PIECE)
    for copy in out:
        copy.wait()


def gather_edges(got_ref, edges_ref):
    owner = lax.broadcasted_iota(jnp.int32, (PIECE, LANES), 1) // 32
    pieces = [got_ref[k, EDGE_ROW:SEND_ROWS, :].astype(F32) for k in range(PEERS)]
    for half in range(2):
        for g in range(ROWS // PIECE):
            total = jnp.zeros((PIECE, LANES), F32)
            for k in range(4):
                turn = 32 * ((k - g) % 4)
                piece = pieces[4 * half + k]
                total = jnp.where(owner == k, pltpu.roll(piece, turn, 1) if turn else piece, total)
            edges_ref[half * ROWS + g * PIECE : half * ROWS + (g + 1) * PIECE, :] = total


def build_halo(to_far, got_ref, edges_ref, out_ref, wide, out):
    core = lax.axis_index("sky") % 2
    last = core if to_far else 1 - core
    for k in range(PEERS):
        wide[k] = got_ref[k, :EDGE_ROW, :].astype(F32)
    for j in range(EPOCHS):
        for a in range(2):
            for t in range(2):
                source = ((a * 2 + j % 2) * 2 + t) * ROWS + last * (ROWS - HALO[j])
                row = (a * 2 + t) * HALO_ROWS + HALO_AT[j]
                out[row : row + HALO[j], :] = wide[j // 2, pl.ds(source, HALO[j]), :]
    out[EDGE_LO_AT:EDGE_HI_AT, :] = edges_ref[pl.ds(last * (ROWS - EDGE_LO), EDGE_LO), :]
    rest = EDGE_HI_AT + EDGE_HI
    out[EDGE_HI_AT:rest, :] = edges_ref[pl.ds(ROWS + last * (ROWS - EDGE_HI), EDGE_HI), :]
    out[rest:HALO_SEND, :] = jnp.zeros((HALO_SEND - rest, LANES), F32)
    out_ref[...] = out[...].astype(BF16)


def halo_kernel(to_far, got_ref, out_ref, edges_ref, wide, out):
    gather_edges(got_ref, edges_ref)
    build_halo(to_far, got_ref, edges_ref, out_ref, wide, out)


def split(values):
    high = values.astype(BF16)
    return high, (values - high.astype(F32)).astype(BF16)


def column_filter(image, variance, image_edge, variance_edge, taps_ref, edge_taps_ref):
    high, low = split(image.astype(F32) * variance.astype(F32))
    edge = image_edge * variance_edge
    edge_high = edge.astype(BF16).astype(F32)
    lane = lax.broadcasted_iota(jnp.int32, edge.shape, 1)
    second = (lane >= REACH) & (lane < REACH + 8)
    third = (lane >= REACH + 8) & (lane < REACH + 16)
    psi_edge = jnp.where(second, pltpu.roll(edge - edge_high, 8, 1), edge_high)
    psi_edge = jnp.where(third, pltpu.roll(edge_high, 16, 1), psi_edge)
    phi_edge = jnp.where(second, pltpu.roll(variance_edge, 8, 1), variance_edge)

    def dot(left, right):
        return jnp.dot(left, right, preferred_element_type=F32)

    psi = dot(high, taps_ref[0]) + (dot(low, taps_ref[0]) + dot(high, taps_ref[1]))
    psi = psi + dot(psi_edge.astype(BF16), edge_taps_ref[0])
    phi = dot(variance, taps_ref[2]) + dot(variance, taps_ref[3])
    phi = phi + dot(phi_edge.astype(BF16), edge_taps_ref[1])
    return psi, phi


def own_kernel(
    cols_ref, got_ref, edges_ref, out_ref, taps_ref, edge_taps_ref, image, variance, image_edge, variance_edge
):
    def terms(height, offset):
        step = lax.broadcasted_iota(jnp.int32, (height, LANES), 0) - lax.broadcasted_iota(
            jnp.int32, (height, LANES), 1
        )
        step = step + (offset + REACH)
        psi_taps = jnp.zeros((height, LANES), F32)
        phi_taps = jnp.zeros((height, LANES), F32)
        for b in range(PSF):
            hit = step == b
            psi_taps = jnp.where(hit, cols_ref[b], psi_taps)
            phi_taps = jnp.where(hit, cols_ref[b] * cols_ref[b], phi_taps)
        return split(psi_taps) + split(phi_taps)

    taps_ref[...] = jnp.zeros(taps_ref.shape, BF16)
    for n, (on, left, right) in enumerate(zip(terms(LANES, 0), terms(16, LANES), terms(16, -16))):
        taps_ref[n, :LANES, :LANES] = on
        taps_ref[n, LANES:, LANES:] = on
        taps_ref[n, LANES : LANES + 16, :LANES] = left
        taps_ref[n, LANES - 16 : LANES, LANES:] = right
    place = lax.broadcasted_iota(jnp.int32, (LANES, COLS), 0)
    place = (place + REACH) % LANES
    part, place = place // 8, place % 8
    source = jnp.where(place < REACH, place - REACH, COLS + place - REACH)
    step = source - lax.broadcasted_iota(jnp.int32, (LANES, COLS), 1) + REACH
    psi_taps = jnp.zeros((LANES, COLS), F32)
    phi_taps = jnp.zeros((LANES, COLS), F32)
    for b in range(PSF):
        hit = step == b
        psi_taps = jnp.where(hit, cols_ref[b], psi_taps)
        phi_taps = jnp.where(hit, cols_ref[b] * cols_ref[b], phi_taps)
    zero = jnp.zeros((LANES, COLS), F32)
    psi_high = psi_taps.astype(BF16).astype(F32)
    phi_high = phi_taps.astype(BF16).astype(F32)
    psi_taps = jnp.where(part < 2, psi_high, jnp.where(part == 2, psi_taps - psi_high, zero))
    phi_taps = jnp.where(part == 0, phi_high, jnp.where(part == 1, phi_taps - phi_high, zero))
    edge_taps_ref[0] = psi_taps.astype(BF16)
    edge_taps_ref[1] = phi_taps.astype(BF16)
    for j in range(EPOCHS):
        rows = slice(j * ROWS, (j + 1) * ROWS)
        for a, (ref, edge_ref) in enumerate(((image, image_edge), (variance, variance_edge))):
            for t in range(2):
                row = ((a * 2 + j % 2) * 2 + t) * ROWS
                ref[rows, t * LANES : (t + 1) * LANES] = got_ref[j // 2, row : row + ROWS, :]
            turn = (LANES - REACH - edge_lane(a, j)) % LANES
            edge_ref[rows, :] = pltpu.roll(edges_ref[j // 8 * ROWS : (j // 8 + 1) * ROWS, :], turn, 1)
    psi, phi = column_filter(
        image[...], variance[...], image_edge[...], variance_edge[...], taps_ref, edge_taps_ref
    )
    for j in range(EPOCHS):
        rows = slice(j * ROWS, (j + 1) * ROWS)
        for t in range(2):
            lanes = slice(t * LANES, (t + 1) * LANES)
            out_ref[j, t] = psi[rows, lanes]
            out_ref[j, 2 + t] = phi[rows, lanes]


def put_halo(above, halo_ref, taps_ref, edge_taps_ref, edges, filtered, maps):
    edges[0, : HALO_SEND - EDGE_LO_AT, :] = halo_ref[EDGE_LO_AT:HALO_SEND, :].astype(F32)
    for a in range(2):
        for j in range(EPOCHS):
            start, height = (0, EDGE_LO) if j < 8 else (EDGE_LO, EDGE_HI)
            start = start + above * (height - HALO[j])
            turn = (LANES - REACH - edge_lane(a, j)) % LANES
            piece = edges[0, pl.ds(start, HALO[j]), :]
            edges[1 + a, HALO_AT[j] : HALO_AT[j] + HALO[j], :] = pltpu.roll(piece, turn, 1)

    def both(a):
        left = halo_ref[2 * a * HALO_ROWS : (2 * a + 1) * HALO_ROWS, :]
        right = halo_ref[(2 * a + 1) * HALO_ROWS : (2 * a + 2) * HALO_ROWS, :]
        return jnp.concatenate([left, right], axis=1)

    psi, phi = column_filter(both(0), both(1), edges[1], edges[2], taps_ref, edge_taps_ref)
    for t in range(2):
        lanes = slice(t * LANES, (t + 1) * LANES)
        filtered[t] = psi[:, lanes]
        filtered[2 + t] = phi[:, lanes]
    for j in range(EPOCHS):
        start = jnp.where(above == 1, BASE - HALO[j], BASE + ROWS)
        for p in range(4):
            maps[j, p, pl.ds(start, HALO[j]), :] = filtered[p, HALO_AT[j] : HALO_AT[j] + HALO[j], :]


def slot(level, j):
    done = j & ((1 << level) - 1)
    if not done:
        return j
    b = done.bit_length() - 1
    return EPOCHS + 8 * b + ((j >> (b + 1)) << b | (j & ((1 << b) - 1)))


def moves(shift_ref, level, j):
    number = shift_ref[level, j]
    whole = lax.shift_right_arithmetic(number, 2)
    part = number - whole * 4
    fraction = part.astype(F32) * 0.25
    behind = jnp.where(part > 0, whole + 1, whole)
    return whole, behind, 1.0 - fraction, fraction


def shifted(ref, place, p, r, height, move):
    whole, behind, keep, fraction = move
    return keep * ref[place, p, pl.ds(r - whole, height), :] + fraction * ref[place, p, pl.ds(r - behind, height), :]


EDGE = [REACH, REACH + 2, REACH + 6, REACH + 14]


def span_of(core, level, reach, far):
    height = EDGE[level] + reach if far else ROWS - EDGE[level] + reach
    count = -(-height // 8)
    top, bottom = BASE + EDGE[level], BASE + ROWS - EDGE[level]
    if far:
        return jnp.where(core == 0, top - 8 * count, bottom), count
    return jnp.where(core == 0, top, bottom - 8 * count), count


def filter_rows(core, far, rows_ref, maps, stacks):
    taps = [[rows_ref[a] for a in range(PSF)], [rows_ref[a] * rows_ref[a] for a in range(PSF)]]
    for j in range(EPOCHS):
        start, count = span_of(core, 0, 2 * j, far)
        for p in range(4):
            factors = taps[p // 2]
            total = factors[0] * maps[j, p, pl.ds(start - REACH, 8 * count), :]
            for a in range(1, PSF):
                total = total + factors[a] * maps[j, p, pl.ds(start - REACH + a, 8 * count), :]
            stacks[j, p, pl.ds(start, 8 * count), :] = total


BATCH = 12


def run_level(core, far, level, shift_ref, stacks):
    held, size = [], 0

    def store():
        for place, p, rows, value in held:
            stacks[place, p, rows, :] = value
        held.clear()

    for low in range(EPOCHS):
        if low >> level & 1:
            continue
        high = low + (1 << level)
        reach = 2 * (low >> (level + 1) << (level + 1))
        start, count = span_of(core, level + 1, reach, far)
        rows = pl.ds(start, 8 * count)
        to_low, to_high = moves(shift_ref, level, low), moves(shift_ref, level, high)
        from_at = slot(level, high)
        for p in range(4):
            if size + count > BATCH:
                store()
                size = 0
            base = stacks[slot(level, low), p, rows, :]
            for place, move in ((slot(level + 1, low), to_low), (slot(level + 1, high), to_high)):
                held.append((place, p, rows, base + shifted(stacks, from_at, p, start, 8 * count, move)))
            size += count
    store()


def inner_kernel(
    rows_ref, shift_ref, own_ref, taps_ref, edge_taps_ref, near_ref, stacks, edges, filtered, maps
):
    core = lax.axis_index("sky") % 2
    put_halo(core, near_ref, taps_ref, edge_taps_ref, edges, filtered, maps)
    for j in range(EPOCHS):
        for p in range(4):
            maps[j, p, BASE : BASE + ROWS, :] = own_ref[j, p]
    filter_rows(core, False, rows_ref, maps, stacks)
    for level in range(LEVELS - 1):
        run_level(core, False, level, shift_ref, stacks)


def outer_kernel(
    rows_ref,
    shift_ref,
    own_ref,
    taps_ref,
    edge_taps_ref,
    far_ref,
    stacks_in,
    out_ref,
    stacks,
    edges,
    filtered,
    maps,
    values,
):
    sky = lax.axis_index("sky")
    sky_last = lax.axis_size("sky") - 1
    core = sky % 2

    def clear(level):
        @pl.when(sky == 0)
        def _():
            for j in range(EPOCHS):
                stacks[slot(level, j), :, :BASE, :] = jnp.zeros((4, BASE, LANES), F32)

        @pl.when(sky == sky_last)
        def _():
            for j in range(EPOCHS):
                stacks[slot(level, j), :, BASE + ROWS :, :] = jnp.zeros((4, SPAN - BASE - ROWS, LANES), F32)

    put_halo(1 - core, far_ref, taps_ref, edge_taps_ref, edges, filtered, maps)
    own_rows = core * (ROWS - 8)
    for j in range(EPOCHS):
        for p in range(4):
            maps[j, p, pl.ds(BASE + own_rows, 8), :] = own_ref[j, p, pl.ds(own_rows, 8), :]
    filter_rows(core, True, rows_ref, maps, stacks)
    clear(0)
    for level in range(LEVELS - 1):
        run_level(core, True, level, shift_ref, stacks)
        clear(level + 1)
    level = LEVELS - 1
    half = 1 << level
    last_moves = [(moves(shift_ref, level, low), moves(shift_ref, level, low + half)) for low in range(half)]
    for t in range(2):
        peak = None
        for low in range(half):
            base_at, from_at = slot(level, low), slot(level, low + half)
            psi_base = stacks[base_at, t, BASE : BASE + ROWS, :]
            phi_base = stacks[base_at, 2 + t, BASE : BASE + ROWS, :]
            for side, move in enumerate(last_moves[low]):
                psi = psi_base + shifted(stacks, from_at, t, BASE, ROWS, move)
                phi = phi_base + shifted(stacks, from_at, 2 + t, BASE, ROWS, move)
                value = psi * lax.rsqrt(phi)
                values[low + side * half] = value
                peak = value if peak is None else jnp.maximum(peak, value)
        total = jnp.exp(values[0] - peak)
        for v in range(1, EPOCHS):
            total = total + jnp.exp(values[v] - peak)
        out_ref[:, t * LANES : (t + 1) * LANES] = peak + jnp.log(total)


SLOTS = EPOCHS + 8 * (LEVELS - 1)


def smem():
    return pl.BlockSpec(memory_space=pltpu.SMEM)


def vmem():
    return pl.BlockSpec(memory_space=pltpu.VMEM)


def limits(mebibytes=32):
    return pltpu.CompilerParams(vmem_limit_bytes=mebibytes * 1024 * 1024)


def cost(microseconds):
    return pl.CostEstimate(flops=microseconds * 1_000_000_000, bytes_accessed=microseconds * 3_000_000, transcendentals=0)


def build(to_far, got, name):
    halo_shape = jax.ShapeDtypeStruct((HALO_SEND, LANES), BF16)
    edge_shape = (2 * ROWS, LANES)
    work = [pltpu.VMEM((PEERS, EDGE_ROW, LANES), F32), pltpu.VMEM((HALO_SEND, LANES), F32)]
    return pl.pallas_call(
        functools.partial(halo_kernel, to_far),
        out_shape=(halo_shape, jax.ShapeDtypeStruct(edge_shape, F32)) if to_far else halo_shape,
        in_specs=[vmem()],
        out_specs=(vmem(), vmem()) if to_far else vmem(),
        scratch_shapes=work if to_far else [pltpu.VMEM(edge_shape, F32), *work],
        compiler_params=limits(),
        cost_estimate=cost(1),
        name=name,
    )(got)


def on_device(image, inv_variance, psf_rows, psf_cols, shift_num):
    sky_count = lax.axis_size("sky")
    cols = image.shape[2]
    packed = pl.pallas_call(
        pack_kernel,
        out_shape=jax.ShapeDtypeStruct((PEERS, SEND_ROWS, LANES), BF16),
        in_specs=[pl.BlockSpec(memory_space=pltpu.HBM), pl.BlockSpec(memory_space=pltpu.HBM)],
        out_specs=pl.BlockSpec(memory_space=pltpu.HBM),
        scratch_shapes=[
            pltpu.VMEM((4, ROWS, cols), BF16),
            pltpu.VMEM((4, PEERS, 2 * ROWS, LANES), BF16),
            pltpu.VMEM((PEERS, ROWS, LANES), F32),
            pltpu.VMEM((PEERS, PIECE, LANES), BF16),
            pltpu.SemaphoreType.DMA((4,)),
            pltpu.SemaphoreType.DMA((5,)),
        ],
        compiler_params=limits(60),
        cost_estimate=cost(2),
        name="pack",
    )(image, inv_variance)
    got = lax.all_to_all(packed, "epoch", 0, 0, tiled=True)
    near = build(False, got, "near")
    far, edges = build(True, got, "far")
    near = lax.ppermute(near, "sky", [(i, i ^ 1) for i in range(sky_count)])
    far = lax.ppermute(far, "sky", [(i, i + 1) if i % 2 else (i, i - 1) for i in range(1, sky_count - 1)])
    own, taps, edge_taps = pl.pallas_call(
        own_kernel,
        out_shape=(
            jax.ShapeDtypeStruct((EPOCHS, 4, ROWS, LANES), F32),
            jax.ShapeDtypeStruct((4, COLS, COLS), BF16),
            jax.ShapeDtypeStruct((2, LANES, COLS), BF16),
        ),
        in_specs=[smem(), vmem(), vmem()],
        out_specs=(vmem(), vmem(), vmem()),
        scratch_shapes=[pltpu.VMEM((EPOCHS * ROWS, COLS), BF16)] * 2 + [pltpu.VMEM((EPOCHS * ROWS, LANES), F32)] * 2,
        compiler_params=limits(),
        cost_estimate=cost(5),
        name="own",
    )(psf_cols, got, edges)
    stacks_shape = jax.ShapeDtypeStruct((SLOTS, 4, SPAN, LANES), F32)
    work = [
        pltpu.VMEM((3, HALO_ROWS, LANES), F32),
        pltpu.VMEM((4, HALO_ROWS, LANES), F32),
        pltpu.VMEM((EPOCHS, 4, SPAN, LANES), F32),
    ]
    stacks = pl.pallas_call(
        inner_kernel,
        out_shape=stacks_shape,
        in_specs=[smem(), smem(), vmem(), vmem(), vmem(), vmem()],
        out_specs=vmem(),
        scratch_shapes=work,
        compiler_params=limits(),
        cost_estimate=cost(5),
        name="inner",
    )(psf_rows, shift_num, own, taps, edge_taps, near)
    out, _ = pl.pallas_call(
        outer_kernel,
        out_shape=(jax.ShapeDtypeStruct((ROWS, COLS), F32), stacks_shape),
        in_specs=[smem(), smem(), vmem(), vmem(), vmem(), vmem(), vmem()],
        out_specs=(vmem(), vmem()),
        scratch_shapes=[*work, pltpu.VMEM((EPOCHS, ROWS, LANES), F32)],
        input_output_aliases={6: 1},
        compiler_params=limits(),
        cost_estimate=cost(5),
        name="outer",
    )(psf_rows, shift_num, own, taps, edge_taps, far, stacks)
    return out


def solution(mesh):
    return jax.shard_map(
        on_device,
        mesh=mesh,
        in_specs=(P("epoch", "sky", None), P("epoch", "sky", None), P(), P(), P()),
        out_specs=P("sky", "epoch"),
        check_vma=False,
    )
```

```python
import functools

import jax
import jax.numpy as jnp
from jax import lax
from jax.experimental import pallas as pl
from jax.experimental.pallas import tpu as pltpu
from jax.sharding import PartitionSpec as P

EPOCHS = 16
LEVELS = 4
PSF = 9
REACH = 4
PEERS = 8
ROWS = 48
LANES = 128
COLS = 256
EDGE_ROW = 8 * ROWS
PIECE = 16
SEND_ROWS = EDGE_ROW + PIECE
HALO = [2 * j + REACH for j in range(EPOCHS)]
HALO_AT = [sum(HALO[:j]) for j in range(EPOCHS)]
HALO_ROWS = sum(HALO)
EDGE_LO = HALO[7]
EDGE_HI = HALO[15]
EDGE_LO_AT = 4 * HALO_ROWS
EDGE_HI_AT = EDGE_LO_AT + EDGE_LO
HALO_SEND = 1280
BASE = 40
SPAN = 128
F32 = jnp.float32
BF16 = jnp.bfloat16


def edge_lane(array, j):
    return 32 * ((j // 2) % 4) + (2 * array + j % 2) * 8


def pack_kernel(image_hbm, variance_hbm, out_hbm, held, blocks, sums, edges, arrived, sent):
    lane = lax.broadcasted_iota(jnp.int32, (ROWS, LANES), 1)
    copies = []
    for a, ref in enumerate((image_hbm, variance_hbm)):
        for i in range(2):
            copies.append(pltpu.make_async_copy(ref.at[i], held.at[2 * a + i], arrived.at[2 * a + i]))
            copies[-1].start()

    def edge(b, c):
        picked = jnp.zeros((ROWS, LANES), F32)
        if c > 0:
            left = held[b, :, (2 * c - 1) * LANES : 2 * c * LANES].astype(F32)
            picked = jnp.where(lane >= LANES - REACH, left, picked)
        if c < PEERS - 1:
            right = held[b, :, (2 * c + 2) * LANES : (2 * c + 3) * LANES].astype(F32)
            picked = jnp.where(lane < REACH, right, picked)
        return pltpu.roll(picked, b * 8 + REACH, 1)

    out = []

    def send(source, n, row, height):
        out.append(pltpu.make_async_copy(source, out_hbm.at[:, pl.ds(row, height), :], sent.at[n]))
        out[-1].start()

    for b in range(4):
        copies[b].wait()
        for c in range(PEERS):
            for t in range(2):
                lanes = slice((2 * c + t) * LANES, (2 * c + t + 1) * LANES)
                blocks[b, c, t * ROWS : (t + 1) * ROWS, :] = held[b, :, lanes]
        send(blocks.at[b], b, 2 * b * ROWS, 2 * ROWS)
        for c in range(PEERS):
            total = edge(b, c)
            if b > 0:
                total = total + sums[c]
            if b < 3:
                sums[c] = total
            else:
                pieces = total[:PIECE]
                for g in range(1, ROWS // PIECE):
                    pieces = pieces + pltpu.roll(total[g * PIECE : (g + 1) * PIECE], 32 * g, 1)
                edges[c] = pieces.astype(BF16)
    send(edges, 4, EDGE_ROW, PIECE)
    for copy in out:
        copy.wait()


def gather_edges(got_ref, edges_ref):
    owner = lax.broadcasted_iota(jnp.int32, (PIECE, LANES), 1) // 32
    pieces = [got_ref[k, EDGE_ROW:SEND_ROWS, :].astype(F32) for k in range(PEERS)]
    for half in range(2):
        for g in range(ROWS // PIECE):
            total = jnp.zeros((PIECE, LANES), F32)
            for k in range(4):
                turn = 32 * ((k - g) % 4)
                piece = pieces[4 * half + k]
                total = jnp.where(owner == k, pltpu.roll(piece, turn, 1) if turn else piece, total)
            edges_ref[half * ROWS + g * PIECE : half * ROWS + (g + 1) * PIECE, :] = total


def build_halo(to_far, got_ref, edges_ref, out_ref, wide, out):
    core = lax.axis_index("sky") % 2
    last = core if to_far else 1 - core
    for k in range(PEERS):
        wide[k] = got_ref[k, :EDGE_ROW, :].astype(F32)
    for j in range(EPOCHS):
        for a in range(2):
            for t in range(2):
                source = ((a * 2 + j % 2) * 2 + t) * ROWS + last * (ROWS - HALO[j])
                row = (a * 2 + t) * HALO_ROWS + HALO_AT[j]
                out[row : row + HALO[j], :] = wide[j // 2, pl.ds(source, HALO[j]), :]
    out[EDGE_LO_AT:EDGE_HI_AT, :] = edges_ref[pl.ds(last * (ROWS - EDGE_LO), EDGE_LO), :]
    rest = EDGE_HI_AT + EDGE_HI
    out[EDGE_HI_AT:rest, :] = edges_ref[pl.ds(ROWS + last * (ROWS - EDGE_HI), EDGE_HI), :]
    out[rest:HALO_SEND, :] = jnp.zeros((HALO_SEND - rest, LANES), F32)
    out_ref[...] = out[...].astype(BF16)


def halo_kernel(to_far, got_ref, out_ref, edges_ref, wide, out):
    gather_edges(got_ref, edges_ref)
    build_halo(to_far, got_ref, edges_ref, out_ref, wide, out)


def split(values):
    high = values.astype(BF16)
    return high, (values - high.astype(F32)).astype(BF16)


def column_filter(image, variance, image_edge, variance_edge, taps_ref, edge_taps_ref):
    high, low = split(image.astype(F32) * variance.astype(F32))
    edge = image_edge * variance_edge
    edge_high = edge.astype(BF16).astype(F32)
    lane = lax.broadcasted_iota(jnp.int32, edge.shape, 1)
    second = (lane >= REACH) & (lane < REACH + 8)
    third = (lane >= REACH + 8) & (lane < REACH + 16)
    psi_edge = jnp.where(second, pltpu.roll(edge - edge_high, 8, 1), edge_high)
    psi_edge = jnp.where(third, pltpu.roll(edge_high, 16, 1), psi_edge)
    phi_edge = jnp.where(second, pltpu.roll(variance_edge, 8, 1), variance_edge)

    def dot(left, right):
        return jnp.dot(left, right, preferred_element_type=F32)

    psi = dot(high, taps_ref[0]) + (dot(low, taps_ref[0]) + dot(high, taps_ref[1]))
    psi = psi + dot(psi_edge.astype(BF16), edge_taps_ref[0])
    phi = dot(variance, taps_ref[2]) + dot(variance, taps_ref[3])
    phi = phi + dot(phi_edge.astype(BF16), edge_taps_ref[1])
    return psi, phi


def own_kernel(
    cols_ref, got_ref, edges_ref, out_ref, taps_ref, edge_taps_ref, image, variance, image_edge, variance_edge
):
    def terms(height, offset):
        step = lax.broadcasted_iota(jnp.int32, (height, LANES), 0) - lax.broadcasted_iota(
            jnp.int32, (height, LANES), 1
        )
        step = step + (offset + REACH)
        psi_taps = jnp.zeros((height, LANES), F32)
        phi_taps = jnp.zeros((height, LANES), F32)
        for b in range(PSF):
            hit = step == b
            psi_taps = jnp.where(hit, cols_ref[b], psi_taps)
            phi_taps = jnp.where(hit, cols_ref[b] * cols_ref[b], phi_taps)
        return split(psi_taps) + split(phi_taps)

    taps_ref[...] = jnp.zeros(taps_ref.shape, BF16)
    for n, (on, left, right) in enumerate(zip(terms(LANES, 0), terms(16, LANES), terms(16, -16))):
        taps_ref[n, :LANES, :LANES] = on
        taps_ref[n, LANES:, LANES:] = on
        taps_ref[n, LANES : LANES + 16, :LANES] = left
        taps_ref[n, LANES - 16 : LANES, LANES:] = right
    place = lax.broadcasted_iota(jnp.int32, (LANES, COLS), 0)
    place = (place + REACH) % LANES
    part, place = place // 8, place % 8
    source = jnp.where(place < REACH, place - REACH, COLS + place - REACH)
    step = source - lax.broadcasted_iota(jnp.int32, (LANES, COLS), 1) + REACH
    psi_taps = jnp.zeros((LANES, COLS), F32)
    phi_taps = jnp.zeros((LANES, COLS), F32)
    for b in range(PSF):
        hit = step == b
        psi_taps = jnp.where(hit, cols_ref[b], psi_taps)
        phi_taps = jnp.where(hit, cols_ref[b] * cols_ref[b], phi_taps)
    zero = jnp.zeros((LANES, COLS), F32)
    psi_high = psi_taps.astype(BF16).astype(F32)
    phi_high = phi_taps.astype(BF16).astype(F32)
    psi_taps = jnp.where(part < 2, psi_high, jnp.where(part == 2, psi_taps - psi_high, zero))
    phi_taps = jnp.where(part == 0, phi_high, jnp.where(part == 1, phi_taps - phi_high, zero))
    edge_taps_ref[0] = psi_taps.astype(BF16)
    edge_taps_ref[1] = phi_taps.astype(BF16)
    for j in range(EPOCHS):
        rows = slice(j * ROWS, (j + 1) * ROWS)
        for a, (ref, edge_ref) in enumerate(((image, image_edge), (variance, variance_edge))):
            for t in range(2):
                row = ((a * 2 + j % 2) * 2 + t) * ROWS
                ref[rows, t * LANES : (t + 1) * LANES] = got_ref[j // 2, row : row + ROWS, :]
            turn = (LANES - REACH - edge_lane(a, j)) % LANES
            edge_ref[rows, :] = pltpu.roll(edges_ref[j // 8 * ROWS : (j // 8 + 1) * ROWS, :], turn, 1)
    psi, phi = column_filter(
        image[...], variance[...], image_edge[...], variance_edge[...], taps_ref, edge_taps_ref
    )
    for j in range(EPOCHS):
        rows = slice(j * ROWS, (j + 1) * ROWS)
        for t in range(2):
            lanes = slice(t * LANES, (t + 1) * LANES)
            out_ref[j, t] = psi[rows, lanes]
            out_ref[j, 2 + t] = phi[rows, lanes]


def put_halo(above, halo_ref, taps_ref, edge_taps_ref, edges, filtered, maps):
    edges[0, : HALO_SEND - EDGE_LO_AT, :] = halo_ref[EDGE_LO_AT:HALO_SEND, :].astype(F32)
    for a in range(2):
        for j in range(EPOCHS):
            start, height = (0, EDGE_LO) if j < 8 else (EDGE_LO, EDGE_HI)
            start = start + above * (height - HALO[j])
            turn = (LANES - REACH - edge_lane(a, j)) % LANES
            piece = edges[0, pl.ds(start, HALO[j]), :]
            edges[1 + a, HALO_AT[j] : HALO_AT[j] + HALO[j], :] = pltpu.roll(piece, turn, 1)

    def both(a):
        left = halo_ref[2 * a * HALO_ROWS : (2 * a + 1) * HALO_ROWS, :]
        right = halo_ref[(2 * a + 1) * HALO_ROWS : (2 * a + 2) * HALO_ROWS, :]
        return jnp.concatenate([left, right], axis=1)

    psi, phi = column_filter(both(0), both(1), edges[1], edges[2], taps_ref, edge_taps_ref)
    for t in range(2):
        lanes = slice(t * LANES, (t + 1) * LANES)
        filtered[t] = psi[:, lanes]
        filtered[2 + t] = phi[:, lanes]
    for j in range(EPOCHS):
        start = jnp.where(above == 1, BASE - HALO[j], BASE + ROWS)
        for p in range(4):
            maps[j, p, pl.ds(start, HALO[j]), :] = filtered[p, HALO_AT[j] : HALO_AT[j] + HALO[j], :]


def slot(level, j):
    done = j & ((1 << level) - 1)
    if not done:
        return j
    b = done.bit_length() - 1
    return EPOCHS + 8 * b + ((j >> (b + 1)) << b | (j & ((1 << b) - 1)))


def moves(shift_ref, level, j):
    number = shift_ref[level, j]
    whole = lax.shift_right_arithmetic(number, 2)
    part = number - whole * 4
    fraction = part.astype(F32) * 0.25
    behind = jnp.where(part > 0, whole + 1, whole)
    return whole, behind, 1.0 - fraction, fraction


def shifted(ref, place, p, r, height, move):
    whole, behind, keep, fraction = move
    return keep * ref[place, p, pl.ds(r - whole, height), :] + fraction * ref[place, p, pl.ds(r - behind, height), :]


EDGE = [REACH, REACH + 2, REACH + 6, REACH + 14]


def span_of(core, level, reach, far):
    height = EDGE[level] + reach if far else ROWS - EDGE[level] + reach
    count = -(-height // 8)
    top, bottom = BASE + EDGE[level], BASE + ROWS - EDGE[level]
    if far:
        return jnp.where(core == 0, top - 8 * count, bottom), count
    return jnp.where(core == 0, top, bottom - 8 * count), count


def filter_rows(core, far, rows_ref, maps, stacks):
    taps = [[rows_ref[a] for a in range(PSF)], [rows_ref[a] * rows_ref[a] for a in range(PSF)]]
    for j in range(EPOCHS):
        start, count = span_of(core, 0, 2 * j, far)
        for p in range(4):
            factors = taps[p // 2]
            total = factors[0] * maps[j, p, pl.ds(start - REACH, 8 * count), :]
            for a in range(1, PSF):
                total = total + factors[a] * maps[j, p, pl.ds(start - REACH + a, 8 * count), :]
            stacks[j, p, pl.ds(start, 8 * count), :] = total


BATCH = 12


def run_level(core, far, level, shift_ref, stacks):
    held, size = [], 0

    def store():
        for place, p, rows, value in held:
            stacks[place, p, rows, :] = value
        held.clear()

    for low in range(EPOCHS):
        if low >> level & 1:
            continue
        high = low + (1 << level)
        reach = 2 * (low >> (level + 1) << (level + 1))
        start, count = span_of(core, level + 1, reach, far)
        rows = pl.ds(start, 8 * count)
        to_low, to_high = moves(shift_ref, level, low), moves(shift_ref, level, high)
        from_at = slot(level, high)
        for p in range(4):
            if size + count > BATCH:
                store()
                size = 0
            base = stacks[slot(level, low), p, rows, :]
            for place, move in ((slot(level + 1, low), to_low), (slot(level + 1, high), to_high)):
                held.append((place, p, rows, base + shifted(stacks, from_at, p, start, 8 * count, move)))
            size += count
    store()


def inner_kernel(
    rows_ref, shift_ref, own_ref, taps_ref, edge_taps_ref, near_ref, stacks, edges, filtered, maps
):
    core = lax.axis_index("sky") % 2
    put_halo(core, near_ref, taps_ref, edge_taps_ref, edges, filtered, maps)
    for j in range(EPOCHS):
        for p in range(4):
            maps[j, p, BASE : BASE + ROWS, :] = own_ref[j, p]
    filter_rows(core, False, rows_ref, maps, stacks)
    for level in range(LEVELS - 1):
        run_level(core, False, level, shift_ref, stacks)


def outer_kernel(
    rows_ref,
    shift_ref,
    own_ref,
    taps_ref,
    edge_taps_ref,
    far_ref,
    stacks_in,
    out_ref,
    stacks,
    edges,
    filtered,
    maps,
    values,
):
    sky = lax.axis_index("sky")
    sky_last = lax.axis_size("sky") - 1
    core = sky % 2

    def clear(level):
        @pl.when(sky == 0)
        def _():
            for j in range(EPOCHS):
                stacks[slot(level, j), :, :BASE, :] = jnp.zeros((4, BASE, LANES), F32)

        @pl.when(sky == sky_last)
        def _():
            for j in range(EPOCHS):
                stacks[slot(level, j), :, BASE + ROWS :, :] = jnp.zeros((4, SPAN - BASE - ROWS, LANES), F32)

    put_halo(1 - core, far_ref, taps_ref, edge_taps_ref, edges, filtered, maps)
    own_rows = core * (ROWS - 8)
    for j in range(EPOCHS):
        for p in range(4):
            maps[j, p, pl.ds(BASE + own_rows, 8), :] = own_ref[j, p, pl.ds(own_rows, 8), :]
    filter_rows(core, True, rows_ref, maps, stacks)
    clear(0)
    for level in range(LEVELS - 1):
        run_level(core, True, level, shift_ref, stacks)
        clear(level + 1)
    level = LEVELS - 1
    half = 1 << level
    last_moves = [(moves(shift_ref, level, low), moves(shift_ref, level, low + half)) for low in range(half)]
    for t in range(2):
        peak = None
        for low in range(half):
            base_at, from_at = slot(level, low), slot(level, low + half)
            psi_base = stacks[base_at, t, BASE : BASE + ROWS, :]
            phi_base = stacks[base_at, 2 + t, BASE : BASE + ROWS, :]
            for side, move in enumerate(last_moves[low]):
                psi = psi_base + shifted(stacks, from_at, t, BASE, ROWS, move)
                phi = phi_base + shifted(stacks, from_at, 2 + t, BASE, ROWS, move)
                value = psi * lax.rsqrt(phi)
                values[low + side * half] = value
                peak = value if peak is None else jnp.maximum(peak, value)
        total = jnp.exp(values[0] - peak)
        for v in range(1, EPOCHS):
            total = total + jnp.exp(values[v] - peak)
        out_ref[:, t * LANES : (t + 1) * LANES] = peak + jnp.log(total)


SLOTS = EPOCHS + 8 * (LEVELS - 1)


def smem():
    return pl.BlockSpec(memory_space=pltpu.SMEM)


def vmem():
    return pl.BlockSpec(memory_space=pltpu.VMEM)


def limits(mebibytes=32):
    return pltpu.CompilerParams(vmem_limit_bytes=mebibytes * 1024 * 1024)


def cost(microseconds):
    return pl.CostEstimate(flops=microseconds * 1_000_000_000, bytes_accessed=microseconds * 3_000_000, transcendentals=0)


def build(to_far, got, name):
    return pl.pallas_call(
        functools.partial(halo_kernel, to_far),
        out_shape=(
            jax.ShapeDtypeStruct((HALO_SEND, LANES), BF16),
            jax.ShapeDtypeStruct((2 * ROWS, LANES), F32),
        ),
        in_specs=[vmem()],
        out_specs=(vmem(), vmem()),
        scratch_shapes=[pltpu.VMEM((PEERS, EDGE_ROW, LANES), F32), pltpu.VMEM((HALO_SEND, LANES), F32)],
        compiler_params=limits(),
        cost_estimate=cost(1),
        name=name,
    )(got)


def on_device(image, inv_variance, psf_rows, psf_cols, shift_num):
    sky_count = lax.axis_size("sky")
    cols = image.shape[2]
    packed = pl.pallas_call(
        pack_kernel,
        out_shape=jax.ShapeDtypeStruct((PEERS, SEND_ROWS, LANES), BF16),
        in_specs=[pl.BlockSpec(memory_space=pltpu.HBM), pl.BlockSpec(memory_space=pltpu.HBM)],
        out_specs=pl.BlockSpec(memory_space=pltpu.HBM),
        scratch_shapes=[
            pltpu.VMEM((4, ROWS, cols), BF16),
            pltpu.VMEM((4, PEERS, 2 * ROWS, LANES), BF16),
            pltpu.VMEM((PEERS, ROWS, LANES), F32),
            pltpu.VMEM((PEERS, PIECE, LANES), BF16),
            pltpu.SemaphoreType.DMA((4,)),
            pltpu.SemaphoreType.DMA((5,)),
        ],
        compiler_params=limits(60),
        cost_estimate=cost(2),
        name="pack",
    )(image, inv_variance)
    got = lax.all_to_all(packed, "epoch", 0, 0, tiled=True)
    near, _ = build(False, got, "near")
    far, edges = build(True, got, "far")
    near = lax.ppermute(near, "sky", [(i, i ^ 1) for i in range(sky_count)])
    far = lax.ppermute(far, "sky", [(i, i + 1) if i % 2 else (i, i - 1) for i in range(1, sky_count - 1)])
    own, taps, edge_taps = pl.pallas_call(
        own_kernel,
        out_shape=(
            jax.ShapeDtypeStruct((EPOCHS, 4, ROWS, LANES), F32),
            jax.ShapeDtypeStruct((4, COLS, COLS), BF16),
            jax.ShapeDtypeStruct((2, LANES, COLS), BF16),
        ),
        in_specs=[smem(), vmem(), vmem()],
        out_specs=(vmem(), vmem(), vmem()),
        scratch_shapes=[pltpu.VMEM((EPOCHS * ROWS, COLS), BF16)] * 2 + [pltpu.VMEM((EPOCHS * ROWS, LANES), F32)] * 2,
        compiler_params=limits(),
        cost_estimate=cost(5),
        name="own",
    )(psf_cols, got, edges)
    stacks_shape = jax.ShapeDtypeStruct((SLOTS, 4, SPAN, LANES), F32)
    work = [
        pltpu.VMEM((3, HALO_ROWS, LANES), F32),
        pltpu.VMEM((4, HALO_ROWS, LANES), F32),
        pltpu.VMEM((EPOCHS, 4, SPAN, LANES), F32),
    ]
    stacks = pl.pallas_call(
        inner_kernel,
        out_shape=stacks_shape,
        in_specs=[smem(), smem(), vmem(), vmem(), vmem(), vmem()],
        out_specs=vmem(),
        scratch_shapes=work,
        compiler_params=limits(),
        cost_estimate=cost(5),
        name="inner",
    )(psf_rows, shift_num, own, taps, edge_taps, near)
    out, _ = pl.pallas_call(
        outer_kernel,
        out_shape=(jax.ShapeDtypeStruct((ROWS, COLS), F32), stacks_shape),
        in_specs=[smem(), smem(), vmem(), vmem(), vmem(), vmem(), vmem()],
        out_specs=(vmem(), vmem()),
        scratch_shapes=[*work, pltpu.VMEM((EPOCHS, ROWS, LANES), F32)],
        input_output_aliases={6: 1},
        compiler_params=limits(),
        cost_estimate=cost(5),
        name="outer",
    )(psf_rows, shift_num, own, taps, edge_taps, far, stacks)
    return out


def solution(mesh):
    return jax.shard_map(
        on_device,
        mesh=mesh,
        in_specs=(P("epoch", "sky", None), P("epoch", "sky", None), P(), P(), P()),
        out_specs=P("sky", "epoch"),
        check_vma=False,
    )
```

```python
import functools

import jax
import jax.numpy as jnp
from jax import lax
from jax.experimental import pallas as pl
from jax.experimental.pallas import tpu as pltpu
from jax.sharding import PartitionSpec as P

EPOCHS = 16
LEVELS = 4
PSF = 9
REACH = 4
PEERS = 8
ROWS = 48
LANES = 128
COLS = 256
EDGE_ROW = 8 * ROWS
PIECE = 16
SEND_ROWS = EDGE_ROW + PIECE
HALO = [2 * j + REACH for j in range(EPOCHS)]
HALO_AT = [sum(HALO[:j]) for j in range(EPOCHS)]
HALO_ROWS = sum(HALO)
EDGE_LO = HALO[7]
EDGE_HI = HALO[15]
EDGE_LO_AT = 4 * HALO_ROWS
EDGE_HI_AT = EDGE_LO_AT + EDGE_LO
HALO_SEND = 1280
BASE = 40
SPAN = 128
F32 = jnp.float32
BF16 = jnp.bfloat16


def edge_lane(array, j):
    return 32 * ((j // 2) % 4) + (2 * array + j % 2) * 8


def pack_kernel(image_hbm, variance_hbm, out_hbm, held, blocks, sums, edges, arrived, sent):
    lane = lax.broadcasted_iota(jnp.int32, (ROWS, LANES), 1)
    copies = []
    for a, ref in enumerate((image_hbm, variance_hbm)):
        for i in range(2):
            copies.append(pltpu.make_async_copy(ref.at[i], held.at[2 * a + i], arrived.at[2 * a + i]))
            copies[-1].start()

    def edge(b, c):
        picked = jnp.zeros((ROWS, LANES), F32)
        if c > 0:
            left = held[b, :, (2 * c - 1) * LANES : 2 * c * LANES].astype(F32)
            picked = jnp.where(lane >= LANES - REACH, left, picked)
        if c < PEERS - 1:
            right = held[b, :, (2 * c + 2) * LANES : (2 * c + 3) * LANES].astype(F32)
            picked = jnp.where(lane < REACH, right, picked)
        return pltpu.roll(picked, b * 8 + REACH, 1)

    out = []

    def send(source, n, row, height):
        out.append(pltpu.make_async_copy(source, out_hbm.at[:, pl.ds(row, height), :], sent.at[n]))
        out[-1].start()

    for b in range(4):
        copies[b].wait()
        for c in range(PEERS):
            for t in range(2):
                lanes = slice((2 * c + t) * LANES, (2 * c + t + 1) * LANES)
                blocks[b, c, t * ROWS : (t + 1) * ROWS, :] = held[b, :, lanes]
        send(blocks.at[b], b, 2 * b * ROWS, 2 * ROWS)
        for c in range(PEERS):
            total = edge(b, c)
            if b > 0:
                total = total + sums[c]
            if b < 3:
                sums[c] = total
            else:
                pieces = total[:PIECE]
                for g in range(1, ROWS // PIECE):
                    pieces = pieces + pltpu.roll(total[g * PIECE : (g + 1) * PIECE], 32 * g, 1)
                edges[c] = pieces.astype(BF16)
    send(edges, 4, EDGE_ROW, PIECE)
    for copy in out:
        copy.wait()


def gather_edges(got_ref, edges_ref):
    owner = lax.broadcasted_iota(jnp.int32, (PIECE, LANES), 1) // 32
    pieces = [got_ref[k, EDGE_ROW:SEND_ROWS, :].astype(F32) for k in range(PEERS)]
    for half in range(2):
        for g in range(ROWS // PIECE):
            total = jnp.zeros((PIECE, LANES), F32)
            for k in range(4):
                turn = 32 * ((k - g) % 4)
                piece = pieces[4 * half + k]
                total = jnp.where(owner == k, pltpu.roll(piece, turn, 1) if turn else piece, total)
            edges_ref[half * ROWS + g * PIECE : half * ROWS + (g + 1) * PIECE, :] = total


def build_halo(to_far, got_ref, edges_ref, out_ref, wide, out):
    core = lax.axis_index("sky") % 2
    last = core if to_far else 1 - core
    for k in range(PEERS):
        wide[k] = got_ref[k, :EDGE_ROW, :].astype(F32)
    for j in range(EPOCHS):
        for a in range(2):
            for t in range(2):
                source = ((a * 2 + j % 2) * 2 + t) * ROWS + last * (ROWS - HALO[j])
                row = (a * 2 + t) * HALO_ROWS + HALO_AT[j]
                out[row : row + HALO[j], :] = wide[j // 2, pl.ds(source, HALO[j]), :]
    out[EDGE_LO_AT:EDGE_HI_AT, :] = edges_ref[pl.ds(last * (ROWS - EDGE_LO), EDGE_LO), :]
    rest = EDGE_HI_AT + EDGE_HI
    out[EDGE_HI_AT:rest, :] = edges_ref[pl.ds(ROWS + last * (ROWS - EDGE_HI), EDGE_HI), :]
    out[rest:HALO_SEND, :] = jnp.zeros((HALO_SEND - rest, LANES), F32)
    out_ref[...] = out[...].astype(BF16)


def halo_kernel(to_far, got_ref, out_ref, edges_ref, wide, out):
    gather_edges(got_ref, edges_ref)
    build_halo(to_far, got_ref, edges_ref, out_ref, wide, out)


def split(values):
    high = values.astype(BF16)
    return high, (values - high.astype(F32)).astype(BF16)


def column_filter(image, variance, image_edge, variance_edge, taps_ref, edge_taps_ref):
    high, low = split(image.astype(F32) * variance.astype(F32))
    edge = image_edge * variance_edge
    edge_high = edge.astype(BF16).astype(F32)
    lane = lax.broadcasted_iota(jnp.int32, edge.shape, 1)
    second = (lane >= REACH) & (lane < REACH + 8)
    third = (lane >= REACH + 8) & (lane < REACH + 16)
    psi_edge = jnp.where(second, pltpu.roll(edge - edge_high, 8, 1), edge_high)
    psi_edge = jnp.where(third, pltpu.roll(edge_high, 16, 1), psi_edge)
    phi_edge = jnp.where(second, pltpu.roll(variance_edge, 8, 1), variance_edge)

    def dot(left, right):
        return jnp.dot(left, right, preferred_element_type=F32)

    psi = dot(high, taps_ref[0]) + (dot(low, taps_ref[0]) + dot(high, taps_ref[1]))
    psi = psi + dot(psi_edge.astype(BF16), edge_taps_ref[0])
    phi = dot(variance, taps_ref[2]) + dot(variance, taps_ref[3])
    phi = phi + dot(phi_edge.astype(BF16), edge_taps_ref[1])
    return psi, phi


def own_kernel(
    cols_ref, got_ref, edges_ref, out_ref, taps_ref, edge_taps_ref, image, variance, image_edge, variance_edge
):
    def terms(height, offset):
        step = lax.broadcasted_iota(jnp.int32, (height, LANES), 0) - lax.broadcasted_iota(
            jnp.int32, (height, LANES), 1
        )
        step = step + (offset + REACH)
        psi_taps = jnp.zeros((height, LANES), F32)
        phi_taps = jnp.zeros((height, LANES), F32)
        for b in range(PSF):
            hit = step == b
            psi_taps = jnp.where(hit, cols_ref[b], psi_taps)
            phi_taps = jnp.where(hit, cols_ref[b] * cols_ref[b], phi_taps)
        return split(psi_taps) + split(phi_taps)

    taps_ref[...] = jnp.zeros(taps_ref.shape, BF16)
    for n, (on, left, right) in enumerate(zip(terms(LANES, 0), terms(16, LANES), terms(16, -16))):
        taps_ref[n, :LANES, :LANES] = on
        taps_ref[n, LANES:, LANES:] = on
        taps_ref[n, LANES : LANES + 16, :LANES] = left
        taps_ref[n, LANES - 16 : LANES, LANES:] = right
    place = lax.broadcasted_iota(jnp.int32, (LANES, COLS), 0)
    place = (place + REACH) % LANES
    part, place = place // 8, place % 8
    source = jnp.where(place < REACH, place - REACH, COLS + place - REACH)
    step = source - lax.broadcasted_iota(jnp.int32, (LANES, COLS), 1) + REACH
    psi_taps = jnp.zeros((LANES, COLS), F32)
    phi_taps = jnp.zeros((LANES, COLS), F32)
    for b in range(PSF):
        hit = step == b
        psi_taps = jnp.where(hit, cols_ref[b], psi_taps)
        phi_taps = jnp.where(hit, cols_ref[b] * cols_ref[b], phi_taps)
    zero = jnp.zeros((LANES, COLS), F32)
    psi_high = psi_taps.astype(BF16).astype(F32)
    phi_high = phi_taps.astype(BF16).astype(F32)
    psi_taps = jnp.where(part < 2, psi_high, jnp.where(part == 2, psi_taps - psi_high, zero))
    phi_taps = jnp.where(part == 0, phi_high, jnp.where(part == 1, phi_taps - phi_high, zero))
    edge_taps_ref[0] = psi_taps.astype(BF16)
    edge_taps_ref[1] = phi_taps.astype(BF16)
    for j in range(EPOCHS):
        rows = slice(j * ROWS, (j + 1) * ROWS)
        for a, (ref, edge_ref) in enumerate(((image, image_edge), (variance, variance_edge))):
            for t in range(2):
                row = ((a * 2 + j % 2) * 2 + t) * ROWS
                ref[rows, t * LANES : (t + 1) * LANES] = got_ref[j // 2, row : row + ROWS, :]
            turn = (LANES - REACH - edge_lane(a, j)) % LANES
            edge_ref[rows, :] = pltpu.roll(edges_ref[j // 8 * ROWS : (j // 8 + 1) * ROWS, :], turn, 1)
    psi, phi = column_filter(
        image[...], variance[...], image_edge[...], variance_edge[...], taps_ref, edge_taps_ref
    )
    for j in range(EPOCHS):
        rows = slice(j * ROWS, (j + 1) * ROWS)
        for t in range(2):
            lanes = slice(t * LANES, (t + 1) * LANES)
            out_ref[j, t] = psi[rows, lanes]
            out_ref[j, 2 + t] = phi[rows, lanes]


def put_halo(above, halo_ref, taps_ref, edge_taps_ref, edges, filtered, maps):
    edges[0, : HALO_SEND - EDGE_LO_AT, :] = halo_ref[EDGE_LO_AT:HALO_SEND, :].astype(F32)
    for a in range(2):
        for j in range(EPOCHS):
            start, height = (0, EDGE_LO) if j < 8 else (EDGE_LO, EDGE_HI)
            start = start + above * (height - HALO[j])
            turn = (LANES - REACH - edge_lane(a, j)) % LANES
            piece = edges[0, pl.ds(start, HALO[j]), :]
            edges[1 + a, HALO_AT[j] : HALO_AT[j] + HALO[j], :] = pltpu.roll(piece, turn, 1)

    def both(a):
        left = halo_ref[2 * a * HALO_ROWS : (2 * a + 1) * HALO_ROWS, :]
        right = halo_ref[(2 * a + 1) * HALO_ROWS : (2 * a + 2) * HALO_ROWS, :]
        return jnp.concatenate([left, right], axis=1)

    psi, phi = column_filter(both(0), both(1), edges[1], edges[2], taps_ref, edge_taps_ref)
    for t in range(2):
        lanes = slice(t * LANES, (t + 1) * LANES)
        filtered[t] = psi[:, lanes]
        filtered[2 + t] = phi[:, lanes]
    for j in range(EPOCHS):
        start = jnp.where(above == 1, BASE - HALO[j], BASE + ROWS)
        for p in range(4):
            maps[j, p, pl.ds(start, HALO[j]), :] = filtered[p, HALO_AT[j] : HALO_AT[j] + HALO[j], :]


def slot(level, j):
    done = j & ((1 << level) - 1)
    if not done:
        return j
    b = done.bit_length() - 1
    return EPOCHS + 8 * b + ((j >> (b + 1)) << b | (j & ((1 << b) - 1)))


def moves(shift_ref, level, j):
    number = shift_ref[level, j]
    whole = lax.shift_right_arithmetic(number, 2)
    part = number - whole * 4
    fraction = part.astype(F32) * 0.25
    behind = jnp.where(part > 0, whole + 1, whole)
    return whole, behind, 1.0 - fraction, fraction


def shifted(ref, place, p, r, height, move):
    whole, behind, keep, fraction = move
    return keep * ref[place, p, pl.ds(r - whole, height), :] + fraction * ref[place, p, pl.ds(r - behind, height), :]


EDGE = [REACH, REACH + 2, REACH + 6, REACH + 14]


def span_of(core, level, reach, far):
    height = EDGE[level] + reach if far else ROWS - EDGE[level] + reach
    count = -(-height // 8)
    top, bottom = BASE + EDGE[level], BASE + ROWS - EDGE[level]
    if far:
        return jnp.where(core == 0, top - 8 * count, bottom), count
    return jnp.where(core == 0, top, bottom - 8 * count), count


def filter_rows(core, far, rows_ref, maps, stacks):
    taps = [[rows_ref[a] for a in range(PSF)], [rows_ref[a] * rows_ref[a] for a in range(PSF)]]
    for j in range(EPOCHS):
        start, count = span_of(core, 0, 2 * j, far)
        for p in range(4):
            factors = taps[p // 2]
            total = factors[0] * maps[j, p, pl.ds(start - REACH, 8 * count), :]
            for a in range(1, PSF):
                total = total + factors[a] * maps[j, p, pl.ds(start - REACH + a, 8 * count), :]
            stacks[j, p, pl.ds(start, 8 * count), :] = total


BATCH = 12


def run_level(core, far, level, shift_ref, stacks):
    held, size = [], 0

    def store():
        for place, p, rows, value in held:
            stacks[place, p, rows, :] = value
        held.clear()

    for low in range(EPOCHS):
        if low >> level & 1:
            continue
        high = low + (1 << level)
        reach = 2 * (low >> (level + 1) << (level + 1))
        start, count = span_of(core, level + 1, reach, far)
        rows = pl.ds(start, 8 * count)
        to_low, to_high = moves(shift_ref, level, low), moves(shift_ref, level, high)
        from_at = slot(level, high)
        for p in range(4):
            if size + count > BATCH:
                store()
                size = 0
            base = stacks[slot(level, low), p, rows, :]
            for place, move in ((slot(level + 1, low), to_low), (slot(level + 1, high), to_high)):
                held.append((place, p, rows, base + shifted(stacks, from_at, p, start, 8 * count, move)))
            size += count
    store()


def finish(start, height, shift_ref, stacks, values, out_ref, out_row):
    level = LEVELS - 1
    half = 1 << level
    rows = pl.ds(start, height)
    all_moves = [(moves(shift_ref, level, low), moves(shift_ref, level, low + half)) for low in range(half)]
    for t in range(2):
        peak = None
        for low in range(half):
            base_at, from_at = slot(level, low), slot(level, low + half)
            psi_base = stacks[base_at, t, rows, :]
            phi_base = stacks[base_at, 2 + t, rows, :]
            for side, move in enumerate(all_moves[low]):
                psi = psi_base + shifted(stacks, from_at, t, start, height, move)
                phi = phi_base + shifted(stacks, from_at, 2 + t, start, height, move)
                value = psi * lax.rsqrt(phi)
                values[low + side * half, :height, :] = value
                peak = value if peak is None else jnp.maximum(peak, value)
        total = jnp.exp(values[0, :height, :] - peak)
        for v in range(1, EPOCHS):
            total = total + jnp.exp(values[v, :height, :] - peak)
        out_ref[pl.ds(out_row, height), t * LANES : (t + 1) * LANES] = peak + jnp.log(total)


def inner_kernel(
    rows_ref, shift_ref, own_ref, taps_ref, edge_taps_ref, near_ref, stacks, ready_ref, edges, filtered, maps, values
):
    core = lax.axis_index("sky") % 2
    put_halo(core, near_ref, taps_ref, edge_taps_ref, edges, filtered, maps)
    for j in range(EPOCHS):
        for p in range(4):
            maps[j, p, BASE : BASE + ROWS, :] = own_ref[j, p]
    filter_rows(core, False, rows_ref, maps, stacks)
    for level in range(LEVELS - 1):
        run_level(core, False, level, shift_ref, stacks)
    finish(BASE + (1 - core) * (ROWS - 8), 8, shift_ref, stacks, values, ready_ref, 0)


def outer_kernel(
    rows_ref,
    shift_ref,
    own_ref,
    taps_ref,
    edge_taps_ref,
    far_ref,
    ready_ref,
    stacks_in,
    out_ref,
    stacks,
    edges,
    filtered,
    maps,
    values,
):
    sky = lax.axis_index("sky")
    sky_last = lax.axis_size("sky") - 1
    core = sky % 2

    def clear(level):
        @pl.when(sky == 0)
        def _():
            for j in range(EPOCHS):
                stacks[slot(level, j), :, :BASE, :] = jnp.zeros((4, BASE, LANES), F32)

        @pl.when(sky == sky_last)
        def _():
            for j in range(EPOCHS):
                stacks[slot(level, j), :, BASE + ROWS :, :] = jnp.zeros((4, SPAN - BASE - ROWS, LANES), F32)

    put_halo(1 - core, far_ref, taps_ref, edge_taps_ref, edges, filtered, maps)
    own_rows = core * (ROWS - 8)
    for j in range(EPOCHS):
        for p in range(4):
            maps[j, p, pl.ds(BASE + own_rows, 8), :] = own_ref[j, p, pl.ds(own_rows, 8), :]
    filter_rows(core, True, rows_ref, maps, stacks)
    clear(0)
    for level in range(LEVELS - 1):
        run_level(core, True, level, shift_ref, stacks)
        clear(level + 1)
    finish(BASE + 8 * core, ROWS - 8, shift_ref, stacks, values, out_ref, 8 * core)
    ready = (1 - core) * (ROWS - 8)
    out_ref[pl.ds(ready, 8), :] = ready_ref[...]


SLOTS = EPOCHS + 8 * (LEVELS - 1)


def smem():
    return pl.BlockSpec(memory_space=pltpu.SMEM)


def vmem():
    return pl.BlockSpec(memory_space=pltpu.VMEM)


def limits(mebibytes=32):
    return pltpu.CompilerParams(vmem_limit_bytes=mebibytes * 1024 * 1024)


def cost(microseconds):
    return pl.CostEstimate(flops=microseconds * 1_000_000_000, bytes_accessed=microseconds * 3_000_000, transcendentals=0)


def build(to_far, got, name):
    return pl.pallas_call(
        functools.partial(halo_kernel, to_far),
        out_shape=(
            jax.ShapeDtypeStruct((HALO_SEND, LANES), BF16),
            jax.ShapeDtypeStruct((2 * ROWS, LANES), F32),
        ),
        in_specs=[vmem()],
        out_specs=(vmem(), vmem()),
        scratch_shapes=[pltpu.VMEM((PEERS, EDGE_ROW, LANES), F32), pltpu.VMEM((HALO_SEND, LANES), F32)],
        compiler_params=limits(),
        cost_estimate=cost(1),
        name=name,
    )(got)


def on_device(image, inv_variance, psf_rows, psf_cols, shift_num):
    sky_count = lax.axis_size("sky")
    cols = image.shape[2]
    packed = pl.pallas_call(
        pack_kernel,
        out_shape=jax.ShapeDtypeStruct((PEERS, SEND_ROWS, LANES), BF16),
        in_specs=[pl.BlockSpec(memory_space=pltpu.HBM), pl.BlockSpec(memory_space=pltpu.HBM)],
        out_specs=pl.BlockSpec(memory_space=pltpu.HBM),
        scratch_shapes=[
            pltpu.VMEM((4, ROWS, cols), BF16),
            pltpu.VMEM((4, PEERS, 2 * ROWS, LANES), BF16),
            pltpu.VMEM((PEERS, ROWS, LANES), F32),
            pltpu.VMEM((PEERS, PIECE, LANES), BF16),
            pltpu.SemaphoreType.DMA((4,)),
            pltpu.SemaphoreType.DMA((5,)),
        ],
        compiler_params=limits(60),
        cost_estimate=cost(2),
        name="pack",
    )(image, inv_variance)
    got = lax.all_to_all(packed, "epoch", 0, 0, tiled=True)
    near, _ = build(False, got, "near")
    far, edges = build(True, got, "far")
    near = lax.ppermute(near, "sky", [(i, i ^ 1) for i in range(sky_count)])
    far = lax.ppermute(far, "sky", [(i, i + 1) if i % 2 else (i, i - 1) for i in range(1, sky_count - 1)])
    own, taps, edge_taps = pl.pallas_call(
        own_kernel,
        out_shape=(
            jax.ShapeDtypeStruct((EPOCHS, 4, ROWS, LANES), F32),
            jax.ShapeDtypeStruct((4, COLS, COLS), BF16),
            jax.ShapeDtypeStruct((2, LANES, COLS), BF16),
        ),
        in_specs=[smem(), vmem(), vmem()],
        out_specs=(vmem(), vmem(), vmem()),
        scratch_shapes=[pltpu.VMEM((EPOCHS * ROWS, COLS), BF16)] * 2 + [pltpu.VMEM((EPOCHS * ROWS, LANES), F32)] * 2,
        compiler_params=limits(),
        cost_estimate=cost(5),
        name="own",
    )(psf_cols, got, edges)
    stacks_shape = jax.ShapeDtypeStruct((SLOTS, 4, SPAN, LANES), F32)
    work = [
        pltpu.VMEM((3, HALO_ROWS, LANES), F32),
        pltpu.VMEM((4, HALO_ROWS, LANES), F32),
        pltpu.VMEM((EPOCHS, 4, SPAN, LANES), F32),
        pltpu.VMEM((EPOCHS, ROWS, LANES), F32),
    ]
    stacks, ready = pl.pallas_call(
        inner_kernel,
        out_shape=(stacks_shape, jax.ShapeDtypeStruct((8, COLS), F32)),
        in_specs=[smem(), smem(), vmem(), vmem(), vmem(), vmem()],
        out_specs=(vmem(), vmem()),
        scratch_shapes=work,
        compiler_params=limits(),
        cost_estimate=cost(5),
        name="inner",
    )(psf_rows, shift_num, own, taps, edge_taps, near)
    out, _ = pl.pallas_call(
        outer_kernel,
        out_shape=(jax.ShapeDtypeStruct((ROWS, COLS), F32), stacks_shape),
        in_specs=[smem(), smem(), vmem(), vmem(), vmem(), vmem(), vmem(), vmem()],
        out_specs=(vmem(), vmem()),
        scratch_shapes=work,
        input_output_aliases={7: 1},
        compiler_params=limits(),
        cost_estimate=cost(5),
        name="outer",
    )(psf_rows, shift_num, own, taps, edge_taps, far, ready, stacks)
    return out


def solution(mesh):
    return jax.shard_map(
        on_device,
        mesh=mesh,
        in_specs=(P("epoch", "sky", None), P("epoch", "sky", None), P(), P(), P()),
        out_specs=P("sky", "epoch"),
        check_vma=False,
    )
```
